512 devices in a mesh: dp: 8 (over x, core), table: 64 (over y, z).
Axes of the slice: x: 4, y: 4, z: 16, core: 2. Of those that a mesh axis runs over, the one named last changes fastest.
Arguments:
- cotangent: bfloat16 [131072, 256], P(('dp', 'table')), may hold values from -1.5 to 1.5
- hot_ids: int32 [131072, 8], P(('dp', 'table')), may hold values from 0 to 2047
- cold_owner: int32 [131072, 4], P(('dp', 'table')), may hold values from 0 to 63, all different within a row; in each aligned block of 256 rows (0 to 255, 256 to 511, ...) at most 24 rows name the same one
- cold_slot: int32 [131072, 4], P(('dp', 'table')), may hold values from 0 to 127
- live_rows: int32 [64], P('table'), may hold values from 128 to 256, as said below
- hot_weight: float32 [2048, 256], P('table'), may hold values from -0.6 to 0.6
- hot_first: float32 [2048, 256], P('table'), may hold values from -1.2 to 1.2
- hot_second: float32 [2048, 256], P('table'), may hold values from 0.001 to 0.1
- cold_weight: float32 [16384, 256], P('table'), may hold values from -0.6 to 0.6
- cold_first: float32 [16384, 256], P('table'), may hold values from -1.2 to 1.2
- cold_second: float32 [16384, 256], P('table'), may hold values from 0.001 to 0.1
Outputs:
- new_hot_weight: float32 [2048, 256], P('table')
- new_hot_first: float32 [2048, 256], P('table')
- new_hot_second: float32 [2048, 256], P('table')
- new_cold_weight: float32 [16384, 256], P('table')
- new_cold_first: float32 [16384, 256], P('table')
- new_cold_second: float32 [16384, 256], P('table')
The draws below stay inside these ranges and needn't reach their ends.
Inputs may be any that keep to these rules, and one draw needn't show every extreme that they name: `cold_owner`: within the samples of one device (aligned blocks of 256 samples) no owner is named more than 24 times; the 4 owners of a sample differ. `cold_slot`: lookups name only the first 128 slots of a window, which lie inside every shard's live rows. `live_rows`: each count is a multiple of 64; some shard uses its whole window and some uses half.
All inputs are finite; a program needn't handle non-finite values.
Results may differ from the reference program's by a relative error of at most 0.0015.
Values may be sent and summed in bfloat16 or wider, within the bound.
A program may use at most 64 MiB of HBM per device.

```python
import math
import jax
import jax.numpy as jnp
import numpy as np
from jax import lax

E = 256
HOT_PER = 8
COLD_PER = 4
STEP = 3
SAMP_DEV = 256
COLD_DEV = 256
HOT = 2048
COLD = 16384
SAMPLES = 131072
CAP = 24
N_DP = 8
N_TABLE = 64


def draw_live_rows(key, part):
    key = jax.random.fold_in(key, 11)
    key_count, key_full, key_half = jax.random.split(key, 3)
    quarter = COLD_DEV // 4
    live = jax.random.randint(key_count, (N_TABLE,), 2, 5) * quarter
    full_shard = jax.random.randint(key_full, (), 0, N_TABLE)
    half_shard = (full_shard + jax.random.randint(key_half, (), 1, N_TABLE)) % N_TABLE
    live = live.at[full_shard].set(COLD_DEV).at[half_shard].set(2 * quarter)
    return live.astype(jnp.int32)


def with_ends(values, rng, low, top_value):
    longest = values.shape.index(max(values.shape))
    spots = []
    for shift in (0, 1):
        where = [jax.random.randint(jax.random.fold_in(rng, axis), (), 0, length) for axis, length in enumerate(values.shape)]
        where[longest] = (where[longest] + shift) % values.shape[longest]
        spots.append(tuple(where))
    return values.at[spots[0]].set(low).at[spots[1]].set(top_value)


def levels(key, shape, shards, least, largest):
    factor_of = 1.0
    for dim, blocks in shards:
        steps = jax.random.uniform(jax.random.fold_in(jax.random.fold_in(key, 6), dim), (blocks,), jnp.float32, least / len(shards), largest / len(shards))
        factor_of = factor_of * jnp.repeat(jnp.exp(steps), shape[dim] // blocks).reshape((-1,) + (1,) * (len(shape) - 1 - dim))
    return factor_of


def rank_bounds(amount, skew):
    loads = [(1 << 20) // math.isqrt(standing ** skew) + 1 for standing in range(1, amount + 1)]
    deviation = 1 + sum(loads) // (1 << 30)
    return np.cumsum(np.array([max(1, weight // deviation) for weight in loads]))


def skewed_ids(key, extent, count, slope):
    table = rank_bounds(count, slope)
    pick = jax.random.randint(jax.random.fold_in(key, 1), extent, 0, int(table[count - 1]))
    rank = jnp.searchsorted(jnp.asarray(table, jnp.int32), pick, side="right")
    return jax.random.permutation(jax.random.fold_in(key, 2), count)[rank].astype(jnp.int32)


def assign_block(rng, own, number, rows, number_of, top, reach, slope):
    order = jax.random.permutation(rng, number_of)
    packed, usual = load_shares(number_of, rows * top, reach, slope, True), load_shares(number_of, rows * top, reach, slope, False)
    places = jnp.arange(number_of)

    def named(tallies, offset_by):
        used = int((tallies > 0).sum())
        fixed = max(1, used // 4)
        passed = fixed + (places - fixed + offset_by * (used - fixed)) % max(1, number_of - fixed)
        return jnp.zeros((number_of,), jnp.int32).at[order[jnp.where(places < fixed, places, passed)]].set(jnp.asarray(tallies, jnp.int32))

    tallies = jnp.where(number % 4 == 0, named(packed, number // 4), named(usual, number - number // 4 - 1))
    mixed = jax.random.permutation(jax.random.fold_in(own, 3), number_of)
    donor, receiver = mixed[0:number_of // 2 * 2:2], mixed[1:number_of // 2 * 2:2]
    room = jnp.minimum(tallies[donor] - 1, reach - tallies[receiver]) // 2
    room = jnp.where((donor == order[0]) | (receiver == order[0]) | (tallies[receiver] == 0), 0, jnp.maximum(room, 0))
    passed = jax.random.randint(jax.random.fold_in(own, 4), (number_of // 2,), 0, 1 << 20) % (room + 1)
    tallies = tallies.at[donor].add(-passed).at[receiver].add(passed)
    members = jnp.searchsorted(jnp.cumsum(tallies), jnp.arange(rows * top), side="right").astype(jnp.int32)
    table = members.reshape(top, rows).T
    table = table[jax.random.permutation(jax.random.fold_in(own, 1), rows)]
    offset_by = jax.random.randint(jax.random.fold_in(own, 2), (rows, 1), 0, top)
    return jnp.take_along_axis(table, (jnp.arange(top)[None, :] + offset_by) % top, axis=1)


def load_shares(number_of, total, reach, skew, full):
    loads = [(1 << 20) // math.isqrt(grade ** skew) + 1 for grade in range(1, number_of + 1)]
    largest = reach if full else min(reach, max(-(-total // number_of), total * loads[0] // sum(loads)))
    least = 1 if total - largest >= number_of - 1 else 0
    given, rest = [largest] + [least] * (number_of - 1), total - largest - least * (number_of - 1)
    while rest > 0:
        candidates = [i for i in range(1, number_of) if given[i] < largest] or [i for i in range(1, number_of) if given[i] < reach]
        mass, remaining = sum([loads[i] for i in candidates]), rest
        for i in candidates:
            extra = min(reach - given[i], max(1, remaining * loads[i] // mass), rest)
            given[i] = given[i] + extra
            rest = rest - extra
    return np.array(given)


def bell_draw(stream_key, shape, scale, most, pieces=(), kind=jnp.bfloat16):
    entries = scale * jax.random.normal(stream_key, shape, jnp.float32)
    if pieces:
        entries = entries * levels(stream_key, shape, pieces, -0.22, 0.18)
    return jnp.clip(entries, -most, most).astype(kind)


def setup_inputs(seed: int = 0) -> dict:
    seeds = jax.random.split(jax.random.key(seed), 12)
    cotangent = bell_draw(seeds[0], (SAMPLES, E), 0.25, 1.5, ((0, 512),))
    hot_ids = with_ends(skewed_ids(seeds[1], (SAMPLES, HOT_PER), HOT, 2), jax.random.fold_in(seeds[1], 3), 0, HOT - 1).astype(jnp.int32)
    cold_owner_keys = jax.random.split(jax.random.fold_in(seeds[2], 1), SAMPLES // SAMP_DEV)
    cold_owner_turns = jax.random.permutation(jax.random.fold_in(seeds[2], 3), SAMPLES // SAMP_DEV)
    cold_owner = jax.vmap(lambda own, number: assign_block(jax.random.fold_in(seeds[2], 2), own, number, SAMP_DEV, N_TABLE, COLD_PER, CAP, 2))(cold_owner_keys, cold_owner_turns).reshape((SAMPLES, COLD_PER))
    cold_slot = with_ends(skewed_ids(seeds[3], (SAMPLES, COLD_PER), COLD_DEV // 2, 2), jax.random.fold_in(seeds[3], 3), 0, (COLD_DEV // 2) - 1).astype(jnp.int32)
    live_rows = draw_live_rows(jax.random.fold_in(seeds[11], 71), 0)
    hot_weight = bell_draw(seeds[5], (HOT, E), 0.1, 0.6, ((0, 64),), jnp.float32)
    hot_first = bell_draw(seeds[6], (HOT, E), 0.2, 1.2, ((0, 64),), jnp.float32)
    hot_second = jnp.clip(jnp.exp(math.log(0.1) - 4.6051702 * jax.random.uniform(seeds[7], (HOT, E), jnp.float32) ** levels(seeds[7], (HOT, E), ((0, 64),), -0.2, 0.2)), 0.001, 0.1)
    cold_weight = bell_draw(seeds[8], (COLD, E), 0.1, 0.6, ((0, 64),), jnp.float32)
    cold_first = bell_draw(seeds[9], (COLD, E), 0.2, 1.2, ((0, 64),), jnp.float32)
    cold_second = jnp.clip(jnp.exp(math.log(0.1) - 4.6051702 * jax.random.uniform(seeds[10], (COLD, E), jnp.float32) ** levels(seeds[10], (COLD, E), ((0, 64),), -0.2, 0.2)), 0.001, 0.1)
    return {"cotangent": cotangent, "hot_ids": hot_ids, "cold_owner": cold_owner, "cold_slot": cold_slot, "live_rows": live_rows, "hot_weight": hot_weight, "hot_first": hot_first, "hot_second": hot_second, "cold_weight": cold_weight, "cold_first": cold_first, "cold_second": cold_second}


BETA_ONE = 0.9
BETA_TWO = 0.999
ADAM_EPS = 1e-08
LEARN_RATE = 0.05
CLIP_NORM = 4.0

def adam_update(weight, moment_one, moment_two, gradient, active):
    row_norm = jnp.sqrt(lax.optimization_barrier(jnp.sum(gradient * gradient, axis=1, keepdims=True)))
    clipped = gradient * (CLIP_NORM / jnp.maximum(row_norm, CLIP_NORM))
    first_new = BETA_ONE * moment_one + (1.0 - BETA_ONE) * clipped
    second_new = BETA_TWO * moment_two + (1.0 - BETA_TWO) * clipped * clipped
    correct_one = 1.0 - BETA_ONE ** STEP
    correct_two = 1.0 - BETA_TWO ** STEP
    stepped = weight - LEARN_RATE * (first_new / correct_one) / (jnp.sqrt(second_new / correct_two) + ADAM_EPS)
    return (jnp.where(active, stepped, weight), jnp.where(active, first_new, moment_one), jnp.where(active, second_new, moment_two))

def reference(cotangent, hot_ids, cold_owner, cold_slot, live_rows, hot_weight, hot_first, hot_second, cold_weight, cold_first, cold_second):
    features = cotangent.shape[1]
    group = cotangent.shape[0] // N_DP
    cold_index = (cold_owner * COLD_DEV + cold_slot).astype(jnp.int32)

    def accumulate(carry, block):
        hot_grad, cold_grad = carry
        rows_now, hot_now, cold_now = block
        values = rows_now.astype(jnp.float32)
        for position in range(HOT_PER):
            hot_grad = hot_grad + jax.ops.segment_sum(values, hot_now[:, position], num_segments=HOT)
        for position in range(COLD_PER):
            cold_grad = cold_grad + jax.ops.segment_sum(values, cold_now[:, position], num_segments=COLD)
        return ((hot_grad, cold_grad), None)
    blocks = (cotangent.reshape(N_DP, group, features), hot_ids.reshape(N_DP, group, HOT_PER), cold_index.reshape(N_DP, group, COLD_PER))
    start = (jnp.zeros((HOT, features), jnp.float32), jnp.zeros((COLD, features), jnp.float32))
    (hot_grad, cold_grad), unused = lax.scan(accumulate, start, blocks)
    hot_active = jnp.ones((HOT, 1), dtype=bool)
    row_index = jnp.arange(COLD, dtype=jnp.int32)
    cold_active = (row_index % COLD_DEV < live_rows[row_index // COLD_DEV])[:, None]
    hot_new = adam_update(hot_weight, hot_first, hot_second, hot_grad, hot_active)
    cold_new = adam_update(cold_weight, cold_first, cold_second, cold_grad, cold_active)
    return (hot_new[0], hot_new[1], hot_new[2], cold_new[0], cold_new[1], cold_new[2])
```

```python
import functools

import jax
import jax.numpy as jnp
from jax import lax
from jax.experimental import pallas as pl
from jax.experimental.pallas import tpu as pltpu
from jax.sharding import PartitionSpec as P

STEP = 3
BETA_ONE = 0.9
BETA_TWO = 0.999
ADAM_EPS = 1e-08
LEARN_RATE = 0.05
CLIP_NORM = 4.0

NX, NC, NY, NZ = 4, 2, 4, 16
SAMP = 256
FEAT = 256
HOT_LOCAL = 32
WINDOW = 256
TOUCHED = 128
NDP = NX * NC
HOT_SHARE = HOT_LOCAL // NDP
COLD_SHARE = TOUCHED // NDP
CHUNKS = 4
PER = NZ // CHUNKS
BLOCK = PER * (COLD_SHARE + HOT_SHARE)
Z_ORDER = [NZ // 2 + n // 2 if n % 2 == 0 else NZ // 2 - 1 - n // 2 for n in range(NZ)]
LOGICAL = pl.DeviceIdType.MESH


def comm_kernel(
    cot_hbm, hot_hbm, owner_hbm, slot_hbm, out,
    hot_in, owner_in, slot_in, ids, cot, slotfor, counts, psum_own, ysend, yrecv, zown, zsend, zrecv, fbuf,
    load_sem, id_send, id_recv, cot_send, fwd_send, cot_recv, y_send, y_recv, z_send, z_recv, f_send, f_recv,
):
    d = lax.axis_index("dp")
    t = lax.axis_index("table")
    x, c = d // NC, d % NC
    y, z = t // NZ, t % NZ

    def dp_peer(k, e):
        core = (1 - c) if e else c
        return (lax.rem(x + k, NX) * NC + core, t)

    def y_peer(r):
        return (d, lax.rem(y + r, NY) * NZ + z)

    def z_peer(r):
        return (d, y * NZ + lax.rem(z + r, NZ))

    dp_offsets = [(k, e) for k in range(NX) for e in range(NC) if (k, e) != (0, 0)]

    barrier = pltpu.get_barrier_semaphore()
    for r in sorted(range(1, NZ), key=lambda r: -min(r, NZ - r)):
        pl.semaphore_signal(barrier, inc=1, device_id=z_peer(r), device_id_type=LOGICAL)
    for r in range(1, NY):
        pl.semaphore_signal(barrier, inc=1, device_id=y_peer(r), device_id_type=LOGICAL)
    for k, e in dp_offsets:
        pl.semaphore_signal(barrier, inc=1, device_id=dp_peer(k, e), device_id_type=LOGICAL)

    loads = [
        pltpu.make_async_copy(hot_hbm, hot_in, load_sem.at[0]),
        pltpu.make_async_copy(owner_hbm, owner_in, load_sem.at[1]),
        pltpu.make_async_copy(slot_hbm, slot_in, load_sem.at[2]),
        pltpu.make_async_copy(cot_hbm, cot.at[0], load_sem.at[3]),
    ]
    for cp in loads:
        cp.start()
    for cp in loads[:3]:
        cp.wait()
    hot = hot_in[...]
    cold = owner_in[...] * TOUCHED + slot_in[...]
    ids[0, 0:4, :] = hot[0:4] + hot[4:8] * 65536
    ids[0, 4:6, :] = cold[0:2] + cold[2:4] * 65536
    ids[0, 6:8, :] = jnp.zeros((2, SAMP), jnp.int32)
    loads[3].wait()

    pl.semaphore_wait(barrier, (NDP - 1) + (NY - 1) + (NZ - 1))

    pending = []
    for k, e in dp_offsets:
        there = ((NX - k) % NX) * NC + e
        cp = pltpu.make_async_remote_copy(
            src_ref=ids.at[0], dst_ref=ids.at[there], send_sem=id_send.at[there], recv_sem=id_recv.at[there],
            device_id=dp_peer(k, e), device_id_type=LOGICAL)
        cp.start()
        pending.append(cp)
    for k in (2, 1, 3):
        there = (NX - k) * NC
        cp = pltpu.make_async_remote_copy(
            src_ref=cot.at[0], dst_ref=cot.at[there], send_sem=cot_send.at[k], recv_sem=cot_recv.at[there],
            device_id=dp_peer(k, 0), device_id_type=LOGICAL)
        cp.start()
        pending.append(cp)

    def forward(dx):
        cp = pltpu.make_async_remote_copy(
            src_ref=cot.at[dx * NC], dst_ref=cot.at[dx * NC + 1], send_sem=fwd_send.at[dx],
            recv_sem=cot_recv.at[dx * NC + 1], device_id=dp_peer(0, 1), device_id_type=LOGICAL)
        cp.start()
        pending.append(cp)

    forward(0)

    def wait_id(g):
        pltpu.make_async_remote_copy(
            src_ref=ids.at[g], dst_ref=ids.at[g], send_sem=id_send.at[g], recv_sem=id_recv.at[g],
            device_id=dp_peer(0, 1), device_id_type=LOGICAL).wait_recv()

    def wait_cot(g):
        pltpu.make_async_remote_copy(
            src_ref=cot.at[g], dst_ref=cot.at[g], send_sem=cot_send.at[0], recv_sem=cot_recv.at[g],
            device_id=dp_peer(0, 1), device_id_type=LOGICAL).wait_recv()

    row = lax.broadcasted_iota(jnp.int32, (NY * NZ, SAMP), 0)
    order = (row // (NY * PER)) * PER + row % PER
    zrel = jnp.where(order % 2 == 0, NZ // 2 + order // 2, NZ // 2 - 1 - order // 2)
    yrel = (row // PER) % NY
    owner_of = ((y + yrel) % NY) * NZ + (z + zrel) % NZ
    slot_row = lax.broadcasted_iota(jnp.int32, (COLD_SHARE, SAMP), 0) + d * COLD_SHARE

    def hot_codes(q, r):
        i = lax.broadcasted_iota(jnp.int32, (PER * HOT_SHARE, SAMP), 0)
        n = q * PER + i // HOT_SHARE
        rel = jnp.where(n % 2 == 0, NZ // 2 + n // 2, NZ // 2 - 1 - n // 2)
        own = ((y + r) % NY) * NZ + (z + rel) % NZ
        return (own * HOT_SHARE + i % HOT_SHARE).astype(jnp.float32).astype(jnp.bfloat16)

    def build(g):
        block = ids[g]
        lo = block & 65535
        hi = block // 65536
        cold_ids = [lo[4:5], lo[5:6], hi[4:5], hi[5:6]]
        value = jnp.full((NY * NZ, SAMP), -1, jnp.int32)
        for v in cold_ids:
            value = jnp.where(v // TOUCHED == owner_of, v % TOUCHED, value)
        slotfor[...] = value
        hot_ids = []
        for half in (lo, hi):
            sub = half[0:4] & (HOT_LOCAL - 1)
            code = (half[0:4] // HOT_LOCAL) * HOT_SHARE + (sub & (HOT_SHARE - 1))
            code = jnp.where(sub // HOT_SHARE == d, code, -1)
            for j in range(4):
                hot_ids.append(jnp.broadcast_to(code[j:j + 1], (PER * HOT_SHARE, SAMP)).astype(jnp.float32).astype(jnp.bfloat16))
        columns = pl.ds(pl.multiple_of(g * SAMP, SAMP), SAMP)
        for q in range(CHUNKS):
            for r in range(NY):
                for k in range(PER):
                    ell = (q * NY + r) * PER + k
                    match = slotfor[ell:ell + 1, :] == slot_row
                    counts[q, pl.ds(r * BLOCK + k * COLD_SHARE, COLD_SHARE), columns] = jnp.where(match, 1.0, 0.0).astype(jnp.bfloat16)
                codes = hot_codes(q, r)
                total = jnp.zeros((PER * HOT_SHARE, SAMP), jnp.bfloat16)
                for v in hot_ids:
                    total = total + jnp.where(v == codes, jnp.bfloat16(1), jnp.bfloat16(0))
                counts[q, pl.ds(r * BLOCK + PER * COLD_SHARE, PER * HOT_SHARE), columns] = total

    def build_step(g, carry):
        @pl.when(g > 0)
        def _():
            wait_id(g)
        build(g)
        return carry

    lax.fori_loop(0, NDP, build_step, 0)

    for dx in (1, 3, 2):
        wait_cot(dx * NC)
        forward(dx)
    for dx in range(NX):
        wait_cot(dx * NC + 1)

    everything = cot[...].reshape(NDP * SAMP, FEAT)
    for q in range(CHUNKS):
        part = jnp.dot(counts[q], everything, preferred_element_type=jnp.float32)
        psum_own[q] = part[0:BLOCK]
        for r in range(1, NY):
            ysend[q, r - 1] = part[r * BLOCK:(r + 1) * BLOCK].astype(jnp.bfloat16)
            cp = pltpu.make_async_remote_copy(
                src_ref=ysend.at[q, r - 1], dst_ref=yrecv.at[q, NY - 1 - r], send_sem=y_send.at[q, r - 1],
                recv_sem=y_recv.at[q, NY - 1 - r], device_id=y_peer(r), device_id_type=LOGICAL)
            cp.start()
            pending.append(cp)

    for q in range(CHUNKS):
        total = psum_own[q]
        for r in range(NY - 1):
            pltpu.make_async_remote_copy(
                src_ref=yrecv.at[q, r], dst_ref=yrecv.at[q, r], send_sem=y_send.at[q, r], recv_sem=y_recv.at[q, r],
                device_id=y_peer(1), device_id_type=LOGICAL).wait_recv()
            total = total + yrecv[q, r].astype(jnp.float32)
        for k in range(PER):
            n = q * PER + k
            rel = Z_ORDER[n]
            cold_part = total[k * COLD_SHARE:(k + 1) * COLD_SHARE]
            base = PER * COLD_SHARE + k * HOT_SHARE
            hot_part = total[base:base + HOT_SHARE]
            packed = [
                cold_part[:, :128],
                cold_part[:, 128:],
                jnp.concatenate([hot_part[:, :128], hot_part[:, 128:], jnp.zeros((8, 128), jnp.float32)], axis=0),
            ]
            for i in range(3):
                if rel == 0:
                    zown[i] = packed[i]
                else:
                    zsend[n, i] = packed[i].astype(jnp.bfloat16)
            if rel:
                there = Z_ORDER.index(NZ - rel)
                cp = pltpu.make_async_remote_copy(
                    src_ref=zsend.at[n], dst_ref=zrecv.at[there], send_sem=z_send.at[n], recv_sem=z_recv.at[there],
                    device_id=z_peer(rel), device_id_type=LOGICAL)
                cp.start()
                pending.append(cp)

    total = [zown[i] for i in range(3)]
    for n in reversed(range(NZ - 1)):
        pltpu.make_async_remote_copy(
            src_ref=zsend.at[n], dst_ref=zrecv.at[n], send_sem=z_send.at[n], recv_sem=z_recv.at[n],
            device_id=z_peer(1), device_id_type=LOGICAL).wait_recv()
        total = [total[i] + zrecv[n, i].astype(jnp.float32) for i in range(3)]
    fbuf[d, 0:16, :] = total[0]
    fbuf[d, 16:32, :] = total[1]
    fbuf[d, 32:40, :] = total[2][0:8]
    for i, (k, e) in enumerate(dp_offsets):
        cp = pltpu.make_async_remote_copy(
            src_ref=fbuf.at[d], dst_ref=fbuf.at[d], send_sem=f_send.at[i], recv_sem=f_recv.at[d],
            device_id=dp_peer(k, e), device_id_type=LOGICAL)
        cp.start()
        pending.append(cp)
    for k, e in dp_offsets:
        sender = dp_peer(k, e)[0]
        pltpu.make_async_remote_copy(
            src_ref=fbuf.at[sender], dst_ref=fbuf.at[sender], send_sem=f_send.at[0], recv_sem=f_recv.at[sender],
            device_id=dp_peer(k, e), device_id_type=LOGICAL).wait_recv()
    out[...] = fbuf[...]
    for cp in pending:
        cp.wait_send()


def adam(weight, one, two, gradient):
    row_norm = jnp.sqrt(jnp.sum(gradient * gradient, axis=1, keepdims=True))
    clipped = gradient * (CLIP_NORM / jnp.maximum(row_norm, CLIP_NORM))
    first = BETA_ONE * one + (1.0 - BETA_ONE) * clipped
    second = BETA_TWO * two + (1.0 - BETA_TWO) * clipped * clipped
    correct_one = 1.0 - BETA_ONE**STEP
    correct_two = 1.0 - BETA_TWO**STEP
    stepped = weight - LEARN_RATE * (first / correct_one) / (jnp.sqrt(second / correct_two) + ADAM_EPS)
    return stepped, first, second


def adam_kernel(live, grads, hw, h1, h2, cw, c1, c2, ohw, oh1, oh2, ocw, oc1, oc2):
    count = live[0]
    for d in range(NDP):
        rows = slice(d * COLD_SHARE, (d + 1) * COLD_SHARE)
        gradient = jnp.concatenate([grads[d, 0:16, :], grads[d, 16:32, :]], axis=1)
        old = (cw[rows, :], c1[rows, :], c2[rows, :])
        new = adam(*old, gradient)
        active = lax.broadcasted_iota(jnp.int32, (COLD_SHARE, FEAT), 0) + d * COLD_SHARE < count
        for ref, a, b in zip((ocw, oc1, oc2), new, old):
            ref[rows, :] = jnp.where(active, a, b)
    left = jnp.concatenate([grads[d, 32:36, :] for d in range(NDP)], axis=0)
    right = jnp.concatenate([grads[d, 36:40, :] for d in range(NDP)], axis=0)
    new = adam(hw[...], h1[...], h2[...], jnp.concatenate([left, right], axis=1))
    for ref, a in zip((ohw, oh1, oh2), new):
        ref[...] = a
    for start in range(TOUCHED, WINDOW, 32):
        rows = slice(start, start + 32)
        old = (cw[rows, :], c1[rows, :], c2[rows, :])
        new = adam(*old, jnp.zeros((32, FEAT), jnp.float32))
        active = lax.broadcasted_iota(jnp.int32, (32, FEAT), 0) + start < count
        for ref, a, b in zip((ocw, oc1, oc2), new, old):
            ref[rows, :] = jnp.where(active, a, b)


def per_device(cotangent, hot_ids, cold_owner, cold_slot, live_rows, hw, h1, h2, cw, c1, c2):
    vmem = pl.BlockSpec(memory_space=pltpu.VMEM)
    anywhere = pl.BlockSpec(memory_space=pl.ANY)
    dma = pltpu.SemaphoreType.DMA
    bf16, f32, i32 = jnp.bfloat16, jnp.float32, jnp.int32
    grads = pl.pallas_call(
        comm_kernel,
        name="gradients",
        out_shape=jax.ShapeDtypeStruct((NDP, 40, 128), f32),
        in_specs=[anywhere] * 4,
        out_specs=vmem,
        scratch_shapes=[
            pltpu.VMEM((8, SAMP), i32),
            pltpu.VMEM((4, SAMP), i32),
            pltpu.VMEM((4, SAMP), i32),
            pltpu.VMEM((NDP, 8, SAMP), i32),
            pltpu.VMEM((NDP, SAMP, FEAT), bf16),
            pltpu.VMEM((NY * NZ, SAMP), i32),
            pltpu.VMEM((CHUNKS, NY * BLOCK, NDP * SAMP), bf16),
            pltpu.VMEM((CHUNKS, BLOCK, FEAT), f32),
            pltpu.VMEM((CHUNKS, NY - 1, BLOCK, FEAT), bf16),
            pltpu.VMEM((CHUNKS, NY - 1, BLOCK, FEAT), bf16),
            pltpu.VMEM((3, 16, 128), f32),
            pltpu.VMEM((NZ, 3, 16, 128), bf16),
            pltpu.VMEM((NZ, 3, 16, 128), bf16),
            pltpu.VMEM((NDP, 40, 128), f32),
            dma((4,)),
            dma((NDP,)),
            dma((NDP,)),
            dma((NX,)),
            dma((NX,)),
            dma((NDP,)),
            dma((CHUNKS, NY - 1)),
            dma((CHUNKS, NY - 1)),
            dma((NZ,)),
            dma((NZ,)),
            dma((NDP,)),
            dma((NDP,)),
        ],
        compiler_params=pltpu.CompilerParams(collective_id=0, has_side_effects=True, vmem_limit_bytes=32 * 1024 * 1024),
    )(cotangent, hot_ids.T, cold_owner.T, cold_slot.T)
    smem = pl.BlockSpec(memory_space=pltpu.SMEM)
    state = (hw, h1, h2, cw, c1, c2)
    return pl.pallas_call(
        adam_kernel,
        name="adam",
        out_shape=[jax.ShapeDtypeStruct(a.shape, a.dtype) for a in state],
        in_specs=[smem] + [vmem] * 7,
        out_specs=[vmem] * 6,
    )(live_rows, grads, *state)


def solution(mesh):
    rows = P(("dp", "table"), None)
    shard = P("table", None)
    return jax.shard_map(
        per_device, mesh=mesh, in_specs=(rows,) * 4 + (P("table"),) + (shard,) * 6, out_specs=(shard,) * 6,
        check_vma=False)
```

```python
import functools

import jax
import jax.numpy as jnp
from jax import lax
from jax.experimental import pallas as pl
from jax.experimental.pallas import tpu as pltpu
from jax.sharding import PartitionSpec as P

STEP = 3
BETA_ONE = 0.9
BETA_TWO = 0.999
ADAM_EPS = 1e-08
LEARN_RATE = 0.05
CLIP_NORM = 4.0

NX, NC, NY, NZ = 4, 2, 4, 16
SAMP = 256
FEAT = 256
HOT_LOCAL = 32
WINDOW = 256
TOUCHED = 128
NDP = NX * NC
HOT_SHARE = HOT_LOCAL // NDP
COLD_SHARE = TOUCHED // NDP
CHUNKS = 4
PER = NZ // CHUNKS
BLOCK = PER * (COLD_SHARE + HOT_SHARE)
Z_ORDER = [NZ // 2 + n // 2 if n % 2 == 0 else NZ // 2 - 1 - n // 2 for n in range(NZ)]
LOGICAL = pl.DeviceIdType.MESH


def comm_kernel(
    cot_hbm, hot_hbm, owner_hbm, slot_hbm, out,
    hot_in, owner_in, slot_in, ids, cot, slotfor, counts, psum_own, ysend, yrecv, zown, zsend, zrecv, fbuf,
    load_sem, id_send, id_recv, cot_send, fwd_send, cot_recv, y_send, y_recv, z_send, z_recv, f_send, f_recv, tokens,
):
    d = lax.axis_index("dp")
    t = lax.axis_index("table")
    x, c = d // NC, d % NC
    y, z = t // NZ, t % NZ

    def dp_peer(k, e):
        core = (1 - c) if e else c
        return (lax.rem(x + k, NX) * NC + core, t)

    def y_peer(r):
        return (d, lax.rem(y + r, NY) * NZ + z)

    def z_peer(r):
        return (d, y * NZ + lax.rem(z + r, NZ))

    dp_offsets = [(k, e) for k in range(NX) for e in range(NC) if (k, e) != (0, 0)]

    barrier = pltpu.get_barrier_semaphore()
    near_z = (1, 2, NZ - 2, NZ - 1)

    loads = [
        pltpu.make_async_copy(hot_hbm, hot_in, load_sem.at[0]),
        pltpu.make_async_copy(owner_hbm, owner_in, load_sem.at[1]),
        pltpu.make_async_copy(slot_hbm, slot_in, load_sem.at[2]),
        pltpu.make_async_copy(cot_hbm, cot.at[0], load_sem.at[3]),
    ]
    for cp in loads:
        cp.start()
    for k, e in dp_offsets:
        pl.semaphore_signal(barrier, inc=1, device_id=dp_peer(k, e), device_id_type=LOGICAL)
    for r in range(1, NY):
        pl.semaphore_signal(barrier, inc=1, device_id=y_peer(r), device_id_type=LOGICAL)
    for r in near_z:
        pl.semaphore_signal(barrier, inc=1, device_id=z_peer(r), device_id_type=LOGICAL)
    for cp in loads[:3]:
        cp.wait()
    hot = hot_in[...]
    cold = owner_in[...] * TOUCHED + slot_in[...]
    ids[0, 0:4, :] = hot[0:4] + hot[4:8] * 65536
    ids[0, 4:6, :] = cold[0:2] + cold[2:4] * 65536
    ids[0, 6:8, :] = jnp.zeros((2, SAMP), jnp.int32)
    pl.semaphore_wait(barrier, (NDP - 1) + (NY - 1) + len(near_z))

    pending = []
    for k, e in dp_offsets:
        there = ((NX - k) % NX) * NC + e
        cp = pltpu.make_async_remote_copy(
            src_ref=ids.at[0], dst_ref=ids.at[there], send_sem=id_send.at[there], recv_sem=id_recv.at[there],
            device_id=dp_peer(k, e), device_id_type=LOGICAL)
        cp.start()
        pending.append(cp)
    for k in (2, 1, 3):
        there = (NX - k) * NC
        cp = pltpu.make_async_remote_copy(
            src_ref=cot_hbm, dst_ref=cot.at[there], send_sem=cot_send.at[k], recv_sem=cot_recv.at[there],
            device_id=dp_peer(k, 0), device_id_type=LOGICAL)
        cp.start()
        pending.append(cp)

    def forward(dx):
        cp = pltpu.make_async_remote_copy(
            src_ref=cot.at[dx * NC], dst_ref=cot.at[dx * NC + 1], send_sem=fwd_send.at[dx],
            recv_sem=cot_recv.at[dx * NC + 1], device_id=dp_peer(0, 1), device_id_type=LOGICAL)
        cp.start()
        pending.append(cp)

    loads[3].wait()
    forward(0)
    for r, i in ((2, 1), (NZ - 2, 0)):
        pl.semaphore_signal(tokens.at[i], inc=1, device_id=z_peer(r), device_id_type=LOGICAL)

    def wait_id(g):
        pltpu.make_async_remote_copy(
            src_ref=ids.at[g], dst_ref=ids.at[g], send_sem=id_send.at[g], recv_sem=id_recv.at[g],
            device_id=dp_peer(0, 1), device_id_type=LOGICAL).wait_recv()

    def wait_cot(g):
        pltpu.make_async_remote_copy(
            src_ref=cot.at[g], dst_ref=cot.at[g], send_sem=cot_send.at[0], recv_sem=cot_recv.at[g],
            device_id=dp_peer(0, 1), device_id_type=LOGICAL).wait_recv()

    row = lax.broadcasted_iota(jnp.int32, (NY * NZ, SAMP), 0)
    order = (row // (NY * PER)) * PER + row % PER
    zrel = jnp.where(order % 2 == 0, NZ // 2 + order // 2, NZ // 2 - 1 - order // 2)
    yrel = (row // PER) % NY
    owner_of = ((y + yrel) % NY) * NZ + (z + zrel) % NZ
    slot_row = lax.broadcasted_iota(jnp.int32, (COLD_SHARE, SAMP), 0) + d * COLD_SHARE

    def hot_codes(q, r):
        i = lax.broadcasted_iota(jnp.int32, (PER * HOT_SHARE, SAMP), 0)
        n = q * PER + i // HOT_SHARE
        rel = jnp.where(n % 2 == 0, NZ // 2 + n // 2, NZ // 2 - 1 - n // 2)
        own = ((y + r) % NY) * NZ + (z + rel) % NZ
        return (own * HOT_SHARE + i % HOT_SHARE).astype(jnp.float32).astype(jnp.bfloat16)

    def build(g):
        block = ids[g]
        lo = block & 65535
        hi = block // 65536
        cold_ids = [lo[4:5], lo[5:6], hi[4:5], hi[5:6]]
        value = jnp.full((NY * NZ, SAMP), -1, jnp.int32)
        for v in cold_ids:
            value = jnp.where(v // TOUCHED == owner_of, v % TOUCHED, value)
        slotfor[...] = value
        hot_ids = []
        for half in (lo, hi):
            sub = half[0:4] & (HOT_LOCAL - 1)
            code = (half[0:4] // HOT_LOCAL) * HOT_SHARE + (sub & (HOT_SHARE - 1))
            code = jnp.where(sub // HOT_SHARE == d, code, -1)
            for j in range(4):
                hot_ids.append(jnp.broadcast_to(code[j:j + 1], (PER * HOT_SHARE, SAMP)).astype(jnp.float32).astype(jnp.bfloat16))
        columns = pl.ds(pl.multiple_of(g * SAMP, SAMP), SAMP)
        for q in range(CHUNKS):
            for r in range(NY):
                for k in range(PER):
                    ell = (q * NY + r) * PER + k
                    match = slotfor[ell:ell + 1, :] == slot_row
                    counts[q, pl.ds(r * BLOCK + k * COLD_SHARE, COLD_SHARE), columns] = jnp.where(match, 1.0, 0.0).astype(jnp.bfloat16)
                codes = hot_codes(q, r)
                total = jnp.zeros((PER * HOT_SHARE, SAMP), jnp.bfloat16)
                for v in hot_ids:
                    total = total + jnp.where(v == codes, jnp.bfloat16(1), jnp.bfloat16(0))
                counts[q, pl.ds(r * BLOCK + PER * COLD_SHARE, PER * HOT_SHARE), columns] = total

    def build_step(g, carry):
        @pl.when(g > 0)
        def _():
            wait_id(g)
        build(g)
        return carry

    lax.fori_loop(0, NDP, build_step, 0)

    for dx in (1, 3, 2):
        wait_cot(dx * NC)
        forward(dx)
    pl.semaphore_wait(tokens.at[0], 1)
    pl.semaphore_wait(tokens.at[1], 1)
    for r, i in ((4, 3), (NZ - 4, 2)):
        pl.semaphore_signal(tokens.at[i], inc=1, device_id=z_peer(r), device_id_type=LOGICAL)
    for dx in range(NX):
        wait_cot(dx * NC + 1)

    everything = cot[...].reshape(NDP * SAMP, FEAT)
    for q in range(CHUNKS):
        part = jnp.dot(counts[q], everything, preferred_element_type=jnp.float32)
        psum_own[q] = part[0:BLOCK]
        for r in range(1, NY):
            ysend[q, r - 1] = part[r * BLOCK:(r + 1) * BLOCK].astype(jnp.bfloat16)
            cp = pltpu.make_async_remote_copy(
                src_ref=ysend.at[q, r - 1], dst_ref=yrecv.at[q, NY - 1 - r], send_sem=y_send.at[q, r - 1],
                recv_sem=y_recv.at[q, NY - 1 - r], device_id=y_peer(r), device_id_type=LOGICAL)
            cp.start()
            pending.append(cp)

    pl.semaphore_wait(tokens.at[2], 1)
    pl.semaphore_wait(tokens.at[3], 1)
    for q in range(CHUNKS):
        total = psum_own[q]
        for r in range(NY - 1):
            pltpu.make_async_remote_copy(
                src_ref=yrecv.at[q, r], dst_ref=yrecv.at[q, r], send_sem=y_send.at[q, r], recv_sem=y_recv.at[q, r],
                device_id=y_peer(1), device_id_type=LOGICAL).wait_recv()
            total = total + yrecv[q, r].astype(jnp.float32)
        for k in range(PER):
            n = q * PER + k
            rel = Z_ORDER[n]
            cold_part = total[k * COLD_SHARE:(k + 1) * COLD_SHARE]
            base = PER * COLD_SHARE + k * HOT_SHARE
            hot_part = total[base:base + HOT_SHARE]
            packed = [
                cold_part[:, :128],
                cold_part[:, 128:],
                jnp.concatenate([hot_part[:, :128], hot_part[:, 128:], jnp.zeros((8, 128), jnp.float32)], axis=0),
            ]
            for i in range(3):
                if rel == 0:
                    zown[i] = packed[i]
                else:
                    zsend[n, i] = packed[i].astype(jnp.bfloat16)
            if rel:
                there = Z_ORDER.index(NZ - rel)
                cp = pltpu.make_async_remote_copy(
                    src_ref=zsend.at[n], dst_ref=zrecv.at[there], send_sem=z_send.at[n], recv_sem=z_recv.at[there],
                    device_id=z_peer(rel), device_id_type=LOGICAL)
                cp.start()
                pending.append(cp)

    total = [zown[i] for i in range(3)]
    for n in reversed(range(NZ - 1)):
        pltpu.make_async_remote_copy(
            src_ref=zsend.at[n], dst_ref=zrecv.at[n], send_sem=z_send.at[n], recv_sem=z_recv.at[n],
            device_id=z_peer(1), device_id_type=LOGICAL).wait_recv()
        total = [total[i] + zrecv[n, i].astype(jnp.float32) for i in range(3)]
    for i in range(3):
        fbuf[d, i] = total[i].astype(jnp.bfloat16)
    for i, (k, e) in enumerate(dp_offsets):
        cp = pltpu.make_async_remote_copy(
            src_ref=fbuf.at[d], dst_ref=fbuf.at[d], send_sem=f_send.at[i], recv_sem=f_recv.at[d],
            device_id=dp_peer(k, e), device_id_type=LOGICAL)
        cp.start()
        pending.append(cp)
    for k, e in dp_offsets:
        sender = dp_peer(k, e)[0]
        pltpu.make_async_remote_copy(
            src_ref=fbuf.at[sender], dst_ref=fbuf.at[sender], send_sem=f_send.at[0], recv_sem=f_recv.at[sender],
            device_id=dp_peer(k, e), device_id_type=LOGICAL).wait_recv()
    out[...] = fbuf[...]
    for cp in pending:
        cp.wait_send()


def adam(weight, one, two, gradient):
    row_norm = jnp.sqrt(jnp.sum(gradient * gradient, axis=1, keepdims=True))
    clipped = gradient * (CLIP_NORM / jnp.maximum(row_norm, CLIP_NORM))
    first = BETA_ONE * one + (1.0 - BETA_ONE) * clipped
    second = BETA_TWO * two + (1.0 - BETA_TWO) * clipped * clipped
    correct_one = 1.0 - BETA_ONE**STEP
    correct_two = 1.0 - BETA_TWO**STEP
    stepped = weight - LEARN_RATE * (first / correct_one) / (jnp.sqrt(second / correct_two) + ADAM_EPS)
    return stepped, first, second


def adam_kernel(live, grads, *refs):
    olds, news, held, made, load_sem, store_sem = refs[0:6], refs[6:12], refs[12:18], refs[18:24], refs[24], refs[25]
    whole = slice(None)
    parts = [(3, slice(TOUCHED, WINDOW)), (0, whole), (3, slice(0, TOUCHED))]
    loads = [
        [pltpu.make_async_copy(olds[a + i].at[rows], held[a + i].at[rows], load_sem.at[p, i]) for i in range(3)]
        for p, (a, rows) in enumerate(parts)
    ]
    stores = [
        [pltpu.make_async_copy(made[a + i].at[rows], news[a + i].at[rows], store_sem.at[p, i]) for i in range(3)]
        for p, (a, rows) in enumerate(parts)
    ]
    for part in loads:
        for cp in part:
            cp.start()
    count = live[0]

    def cold(rows, start, gradient):
        old = [held[3 + i][rows, :] for i in range(3)]
        new = adam(*old, gradient)
        active = lax.broadcasted_iota(jnp.int32, gradient.shape, 0) + start < count
        for i in range(3):
            made[3 + i][rows, :] = jnp.where(active, new[i], old[i])

    for cp in loads[0]:
        cp.wait()
    for start in range(TOUCHED, WINDOW, 32):
        cold(slice(start, start + 32), start, jnp.zeros((32, FEAT), jnp.float32))
    for cp in stores[0]:
        cp.start()

    for cp in loads[1]:
        cp.wait()
    tiles = [grads[d, 2].astype(jnp.float32) for d in range(NDP)]
    left = jnp.concatenate([tile[0:HOT_SHARE] for tile in tiles], axis=0)
    right = jnp.concatenate([tile[HOT_SHARE:2 * HOT_SHARE] for tile in tiles], axis=0)
    new = adam(held[0][...], held[1][...], held[2][...], jnp.concatenate([left, right], axis=1))
    for i in range(3):
        made[i][...] = new[i]
    for cp in stores[1]:
        cp.start()

    for cp in loads[2]:
        cp.wait()
    for d in range(NDP):
        gradient = jnp.concatenate([grads[d, 0], grads[d, 1]], axis=1).astype(jnp.float32)
        cold(slice(d * COLD_SHARE, (d + 1) * COLD_SHARE), d * COLD_SHARE, gradient)
    for cp in stores[2]:
        cp.start()
    for part in stores:
        for cp in part:
            cp.wait()


def in_hbm(array):
    return pltpu.with_memory_space_constraint(array, pltpu.HBM)


def per_device(cotangent, hot_ids, cold_owner, cold_slot, live_rows, hw, h1, h2, cw, c1, c2):
    vmem = pl.BlockSpec(memory_space=pltpu.VMEM)
    hbm = pl.BlockSpec(memory_space=pltpu.HBM)
    dma = pltpu.SemaphoreType.DMA
    bf16, f32, i32 = jnp.bfloat16, jnp.float32, jnp.int32
    grads = pl.pallas_call(
        comm_kernel,
        name="gradients",
        out_shape=jax.ShapeDtypeStruct((NDP, 3, 16, 128), bf16),
        in_specs=[hbm] * 4,
        out_specs=vmem,
        scratch_shapes=[
            pltpu.VMEM((8, SAMP), i32),
            pltpu.VMEM((4, SAMP), i32),
            pltpu.VMEM((4, SAMP), i32),
            pltpu.VMEM((NDP, 8, SAMP), i32),
            pltpu.VMEM((NDP, SAMP, FEAT), bf16),
            pltpu.VMEM((NY * NZ, SAMP), i32),
            pltpu.VMEM((CHUNKS, NY * BLOCK, NDP * SAMP), bf16),
            pltpu.VMEM((CHUNKS, BLOCK, FEAT), f32),
            pltpu.VMEM((CHUNKS, NY - 1, BLOCK, FEAT), bf16),
            pltpu.VMEM((CHUNKS, NY - 1, BLOCK, FEAT), bf16),
            pltpu.VMEM((3, 16, 128), f32),
            pltpu.VMEM((NZ, 3, 16, 128), bf16),
            pltpu.VMEM((NZ, 3, 16, 128), bf16),
            pltpu.VMEM((NDP, 3, 16, 128), bf16),
            dma((4,)),
            dma((NDP,)),
            dma((NDP,)),
            dma((NX,)),
            dma((NX,)),
            dma((NDP,)),
            dma((CHUNKS, NY - 1)),
            dma((CHUNKS, NY - 1)),
            dma((NZ,)),
            dma((NZ,)),
            dma((NDP,)),
            dma((NDP,)),
            pltpu.SemaphoreType.REGULAR((4,)),
        ],
        compiler_params=pltpu.CompilerParams(collective_id=0, has_side_effects=True, vmem_limit_bytes=32 * 1024 * 1024),
    )(in_hbm(cotangent), in_hbm(hot_ids.T), in_hbm(cold_owner.T), in_hbm(cold_slot.T))
    smem = pl.BlockSpec(memory_space=pltpu.SMEM)
    state = (hw, h1, h2, cw, c1, c2)
    return pl.pallas_call(
        adam_kernel,
        name="adam",
        out_shape=[jax.ShapeDtypeStruct(a.shape, a.dtype) for a in state],
        in_specs=[smem, vmem] + [hbm] * 6,
        out_specs=[hbm] * 6,
        scratch_shapes=[pltpu.VMEM(a.shape, a.dtype) for a in state * 2] + [dma((3, 3)), dma((3, 3))],
    )(live_rows, pltpu.with_memory_space_constraint(grads, pltpu.VMEM), *(in_hbm(a) for a in state))


def solution(mesh):
    rows = P(("dp", "table"), None)
    shard = P("table", None)
    return jax.shard_map(
        per_device, mesh=mesh, in_specs=(rows,) * 4 + (P("table"),) + (shard,) * 6, out_specs=(shard,) * 6,
        check_vma=False)
```

```python
import functools

import jax
import jax.numpy as jnp
from jax import lax
from jax.experimental import pallas as pl
from jax.experimental.pallas import tpu as pltpu
from jax.sharding import PartitionSpec as P

STEP = 3
BETA_ONE = 0.9
BETA_TWO = 0.999
ADAM_EPS = 1e-08
LEARN_RATE = 0.05
CLIP_NORM = 4.0

NX, NC, NY, NZ = 4, 2, 4, 16
SAMP = 256
FEAT = 256
HALF = FEAT // 2
HOT_LOCAL = 32
WINDOW = 256
TOUCHED = 128
NDP = NX * NC
HOT_SHARE = HOT_LOCAL // NDP
COLD_SHARE = TOUCHED // NDP
CHUNKS = 4
PER = NZ // CHUNKS
BLOCK = PER * (COLD_SHARE + HOT_SHARE)
Z_ORDER = [NZ // 2 + n // 2 if n % 2 == 0 else NZ // 2 - 1 - n // 2 for n in range(NZ)]
FOLD = 4
FAR = [r for r in Z_ORDER if FOLD < r < NZ - FOLD]
KEPT = [0, FOLD, NZ - FOLD]
LOGICAL = pl.DeviceIdType.MESH


def comm_kernel(
    cot_hbm, hot_hbm, owner_hbm, slot_hbm, s0, s1, s2, s3, s4, s5, out, o0, o1, o2, o3, o4, o5,
    hot_in, owner_in, slot_in, ids, cot, owner_rows, code_rows, slotfor, counts, part, psum_own, rsend, rrecv, zown,
    zsend, zrecv, zfar, fbuf,
    load_sem, state_sem, id_send, id_recv, cot_send, fwd_send, cot_recv, r_send, r_recv, z_send, z_recv, far_recv, f_send, f_recv,
    tokens,
):
    d = lax.axis_index("dp")
    t = lax.axis_index("table")
    x, c = d // NC, d % NC
    y, z = t // NZ, t % NZ

    def peer(axis, k, e=0):
        core = (1 - c) if e else c
        if axis == 0:
            return (lax.rem(x + k, NX) * NC + core, t)
        return (x * NC + core, lax.rem(y + k, NY) * NZ + z)

    def z_peer(r):
        return (d, y * NZ + lax.rem(z + r, NZ))

    partner = peer(0, 0, 1)
    offsets = [(k, e) for k in (2, 1, 3) for e in range(NC)]
    dp_peers = [partner] + [peer(0, k, e) for k, e in offsets]
    pending = []

    def send(src, dst, send_sem, recv_sem, device):
        cp = pltpu.make_async_remote_copy(
            src_ref=src, dst_ref=dst, send_sem=send_sem, recv_sem=recv_sem, device_id=device, device_id_type=LOGICAL)
        cp.start()
        pending.append(cp)

    def arrive(ref, recv_sem):
        pltpu.make_async_remote_copy(
            src_ref=ref, dst_ref=ref, send_sem=f_send.at[0], recv_sem=recv_sem, device_id=partner,
            device_id_type=LOGICAL).wait_recv()

    def signal(semaphore, device):
        pl.semaphore_signal(semaphore, inc=1, device_id=device, device_id_type=LOGICAL)

    loads = [
        pltpu.make_async_copy(hot_hbm, hot_in, load_sem.at[0]),
        pltpu.make_async_copy(owner_hbm, owner_in, load_sem.at[1]),
        pltpu.make_async_copy(slot_hbm, slot_in, load_sem.at[2]),
    ] + [
        pltpu.make_async_copy(cot_hbm.at[:, pl.ds(h * HALF, HALF)], cot.at[h, 0], load_sem.at[3 + h]) for h in range(2)
    ]
    for cp in loads:
        cp.start()
    barrier = pltpu.get_barrier_semaphore()
    near = [partner] + [peer(h, k) for h in range(2) for k in (2, 1, 3)] + [z_peer(r) for r in (1, 2, NZ - 2, NZ - 1)]
    for device in near:
        signal(barrier, device)
    states = [
        pltpu.make_async_copy(a, b, state_sem.at[i])
        for i, (a, b) in enumerate(zip((s0, s1, s2, s3, s4, s5), (o0, o1, o2, o3, o4, o5)))
    ]
    for cp in states:
        cp.start()

    row = lax.broadcasted_iota(jnp.int32, (NY * NZ, SAMP), 0)
    order = (row // (NY * PER)) * PER + row % PER
    zrel = jnp.where(order % 2 == 0, NZ // 2 + order // 2, NZ // 2 - 1 - order // 2)
    yrel = (row // PER) % NY
    owner_rows[0] = ((y + yrel) % NY) * NZ + (z + zrel) % NZ
    owner_rows[1] = y * NZ + (z + zrel) % NZ
    i = lax.broadcasted_iota(jnp.int32, (PER * HOT_SHARE, SAMP), 0)
    for q in range(CHUNKS):
        n = q * PER + i // HOT_SHARE
        rel = jnp.where(n % 2 == 0, NZ // 2 + n // 2, NZ // 2 - 1 - n // 2)
        zz = (z + rel) % NZ
        for r in range(NY):
            first = (((y + r) % NY) * NZ + zz) * HOT_SHARE + i % HOT_SHARE
            second = (zz * NX + (x + r) % NX) * HOT_SHARE + i % HOT_SHARE
            code_rows[0, q, r] = first.astype(jnp.float32).astype(jnp.bfloat16)
            code_rows[1, q, r] = second.astype(jnp.float32).astype(jnp.bfloat16)
    lanes = lax.broadcasted_iota(jnp.int32, (COLD_SHARE, SAMP), 0)

    def build(h, source, g):
        block = ids[source, g]
        lo = block & 65535
        hi = block // 65536
        value = jnp.full((NY * NZ, SAMP), -1, jnp.int32)
        owners = owner_rows[h]
        for v in (lo[4:5], lo[5:6], hi[4:5], hi[5:6]):
            value = jnp.where(v // TOUCHED == owners, v % TOUCHED, value)
        slotfor[...] = value
        hot_ids = []
        for words in (lo, hi):
            shard = words[0:4] // HOT_LOCAL
            share = (words[0:4] % HOT_LOCAL) // HOT_SHARE
            inner = words[0:4] % HOT_SHARE
            if h == 0:
                code = jnp.where(share == d, shard * HOT_SHARE + inner, -1)
            else:
                code = ((shard % NZ) * NX + share // NC) * HOT_SHARE + inner
                code = jnp.where((shard // NZ == y) & (share % NC == c), code, -1)
            for j in range(4):
                wide = jnp.broadcast_to(code[j:j + 1], (PER * HOT_SHARE, SAMP))
                hot_ids.append(wide.astype(jnp.float32).astype(jnp.bfloat16))
        columns = pl.ds(pl.multiple_of(g * SAMP, SAMP), SAMP)
        for q in range(CHUNKS):
            for r in range(NY):
                share = d if h == 0 else lax.rem(x + r, NX) * NC + c
                slots = lanes + share * COLD_SHARE
                for k in range(PER):
                    ell = (q * NY + r) * PER + k
                    match = slotfor[ell:ell + 1, :] == slots
                    counts[h, q, pl.ds(r * BLOCK + k * COLD_SHARE, COLD_SHARE), columns] = jnp.where(match, 1.0, 0.0).astype(jnp.bfloat16)
                codes = code_rows[h, q, r]
                total = jnp.zeros((PER * HOT_SHARE, SAMP), jnp.bfloat16)
                for v in hot_ids:
                    total = total + jnp.where(v == codes, jnp.bfloat16(1), jnp.bfloat16(0))
                counts[h, q, pl.ds(r * BLOCK + PER * COLD_SHARE, PER * HOT_SHARE), columns] = total

    for cp in loads[:3]:
        cp.wait()
    hot = hot_in[...]
    cold = owner_in[...] * TOUCHED + slot_in[...]
    ids[0, 0, 0:4, :] = hot[0:4] + hot[4:8] * 65536
    ids[0, 0, 4:6, :] = cold[0:2] + cold[2:4] * 65536
    ids[0, 0, 6:8, :] = jnp.zeros((2, SAMP), jnp.int32)
    for cp in loads[3:]:
        cp.wait()
    for h in range(2):
        build(h, 0, 0)

    pl.semaphore_wait(barrier, len(near))

    send(ids.at[0, 0], ids.at[0, NX], id_send.at[0, NX], id_recv.at[0, NX], partner)
    for k in (2, 1, 3):
        for h in range(2):
            send(ids.at[0, 0], ids.at[h, NX - k], id_send.at[h, NX - k], id_recv.at[h, NX - k], peer(h, k))

    def forward(h, k):
        send(cot.at[h, k], cot.at[h, NX + k], fwd_send.at[h, k], cot_recv.at[h, NX + k], partner)

    for k in (2, 1, 3):
        for h in range(2):
            send(cot.at[h, 0], cot.at[h, NX - k], cot_send.at[h, k], cot_recv.at[h, NX - k], peer(h, k))
    for h in range(2):
        forward(h, 0)
    for r, i in ((2, 1), (NZ - 2, 0)):
        signal(tokens.at[i], z_peer(r))

    arrive(ids.at[0, NX], id_recv.at[0, NX])
    for h in range(2):
        build(h, 0, NX)
    for k in (1, 3, 2):
        for h in range(2):
            arrive(ids.at[h, k], id_recv.at[h, k])
            send(ids.at[h, k], ids.at[h, NX + k], id_send.at[h, NX + k], id_recv.at[h, NX + k], partner)

    for h in range(2):
        def build_mine(k, carry):
            build(h, h, k)
            return carry

        lax.fori_loop(1, NX, build_mine, 0)
    for h in range(2):
        def build_other(k, carry):
            arrive(ids.at[h, NX + k], id_recv.at[h, NX + k])
            build(h, h, NX + k)
            return carry

        lax.fori_loop(1, NX, build_other, 0)

    for k in (1, 3, 2):
        for h in range(2):
            arrive(cot.at[h, k], cot_recv.at[h, k])
            forward(h, k)

    middle = NX * SAMP
    for h in range(2):
        mine = cot[h, 0:NX].reshape(middle, HALF)
        for q in range(CHUNKS):
            part[h, q] = jnp.dot(counts[h, q, :, 0:middle], mine, preferred_element_type=jnp.float32)
    for h in range(2):
        for k in (0, 1, 3, 2):
            arrive(cot.at[h, NX + k], cot_recv.at[h, NX + k])
    for q in range(CHUNKS):
        for h in range(2):
            others = cot[h, NX:NDP].reshape(middle, HALF)
            done = part[h, q] + jnp.dot(counts[h, q, :, middle:2 * middle], others, preferred_element_type=jnp.float32)
            psum_own[h, q] = done[0:BLOCK]
            for r in (2, 1, 3):
                rsend[h, q, r - 1] = done[r * BLOCK:(r + 1) * BLOCK].astype(jnp.bfloat16)
                there = NY - 1 - r
                send(rsend.at[h, q, r - 1], rrecv.at[h, q, there], r_send.at[h, q, r - 1], r_recv.at[h, q, there], peer(1 - h, r))

    pl.semaphore_wait(tokens.at[0], 1)
    pl.semaphore_wait(tokens.at[1], 1)
    for q in range(CHUNKS):
        totals = []
        for h in range(2):
            total = psum_own[h, q]
            for r in (0, 2, 1):
                arrive(rrecv.at[h, q, r], r_recv.at[h, q, r])
                total = total + rrecv[h, q, r].astype(jnp.float32)
            totals.append(total)
        for k in range(PER):
            n = q * PER + k
            rel = Z_ORDER[n]
            cold_rows = slice(k * COLD_SHARE, (k + 1) * COLD_SHARE)
            base = PER * COLD_SHARE + k * HOT_SHARE
            hot_parts = [total[base:base + HOT_SHARE] for total in totals]
            packed = [total[cold_rows] for total in totals] + [
                jnp.concatenate(hot_parts + [jnp.zeros((8, HALF), jnp.float32)], axis=0)]
            if rel in KEPT:
                for i in range(3):
                    zown[KEPT.index(rel), i] = packed[i]
                continue
            for i in range(3):
                zsend[n, i] = packed[i].astype(jnp.bfloat16)
            if rel in FAR:
                send(zsend.at[n], zfar.at[FAR.index(rel)], z_send.at[n], far_recv.at[FAR.index(rel)],
                     z_peer(rel - FOLD if rel <= NZ // 2 else rel + FOLD))
            else:
                there = Z_ORDER.index(NZ - rel)
                send(zsend.at[n], zrecv.at[there], z_send.at[n], z_recv.at[there], z_peer(rel))

    for rel in (FOLD, NZ - FOLD):
        total = [zown[KEPT.index(rel), i] for i in range(3)]
        for far in FAR:
            if (far <= NZ // 2) == (rel == FOLD):
                arrive(zfar.at[FAR.index(far)], far_recv.at[FAR.index(far)])
                total = [total[i] + zfar[FAR.index(far), i].astype(jnp.float32) for i in range(3)]
        n, there = Z_ORDER.index(rel), Z_ORDER.index(NZ - rel)
        for i in range(3):
            zsend[n, i] = total[i].astype(jnp.bfloat16)
        send(zsend.at[n], zrecv.at[there], z_send.at[n], z_recv.at[there], z_peer(rel))
    while pending:
        pending.pop(0).wait_send()

    total = [zown[0, i] for i in range(3)]
    for rel in (1, NZ - 1, 2, NZ - 2, 3, NZ - 3, FOLD, NZ - FOLD):
        n = Z_ORDER.index(rel)
        arrive(zrecv.at[n], z_recv.at[n])
        total = [total[i] + zrecv[n, i].astype(jnp.float32) for i in range(3)]
    for i in range(3):
        fbuf[d, i] = total[i].astype(jnp.bfloat16)
    for i, device in enumerate(dp_peers):
        send(fbuf.at[d], fbuf.at[d], f_send.at[i], f_recv.at[d], device)
    for cp in states:
        cp.wait()
    for device in dp_peers:
        arrive(fbuf.at[device[0]], f_recv.at[device[0]])
    out[...] = fbuf[...]
    for cp in pending:
        cp.wait_send()


def adam(weight, one, two, gradient):
    row_norm = jnp.sqrt(jnp.sum(gradient * gradient, axis=1, keepdims=True))
    clipped = gradient * (CLIP_NORM / jnp.maximum(row_norm, CLIP_NORM))
    first = BETA_ONE * one + (1.0 - BETA_ONE) * clipped
    second = BETA_TWO * two + (1.0 - BETA_TWO) * clipped * clipped
    correct_one = 1.0 - BETA_ONE**STEP
    correct_two = 1.0 - BETA_TWO**STEP
    stepped = weight - LEARN_RATE * (first / correct_one) / (jnp.sqrt(second / correct_two) + ADAM_EPS)
    return stepped, first, second


def adam_kernel(live, grads, *refs):
    held, news, made, store_sem = refs[0:6], refs[6:12], refs[12:18], refs[18]
    whole = slice(None)
    parts = [(3, slice(TOUCHED, WINDOW)), (0, whole), (3, slice(0, TOUCHED))]
    stores = [
        [pltpu.make_async_copy(made[a + i].at[rows], news[a + i].at[rows], store_sem.at[p, i]) for i in range(3)]
        for p, (a, rows) in enumerate(parts)
    ]
    count = live[0]

    def cold(rows, start, gradient):
        old = [held[3 + i][rows, :] for i in range(3)]
        new = adam(*old, gradient)
        active = lax.broadcasted_iota(jnp.int32, gradient.shape, 0) + start < count
        for i in range(3):
            made[3 + i][rows, :] = jnp.where(active, new[i], old[i])

    for start in range(TOUCHED, WINDOW, 32):
        cold(slice(start, start + 32), start, jnp.zeros((32, FEAT), jnp.float32))
    for cp in stores[0]:
        cp.start()

    tiles = [grads[d, 2].astype(jnp.float32) for d in range(NDP)]
    left = jnp.concatenate([tile[0:HOT_SHARE] for tile in tiles], axis=0)
    right = jnp.concatenate([tile[HOT_SHARE:2 * HOT_SHARE] for tile in tiles], axis=0)
    new = adam(held[0][...], held[1][...], held[2][...], jnp.concatenate([left, right], axis=1))
    for i in range(3):
        made[i][...] = new[i]
    for cp in stores[1]:
        cp.start()

    for d in range(NDP):
        gradient = jnp.concatenate([grads[d, 0], grads[d, 1]], axis=1).astype(jnp.float32)
        cold(slice(d * COLD_SHARE, (d + 1) * COLD_SHARE), d * COLD_SHARE, gradient)
    for cp in stores[2]:
        cp.start()
    for part in stores:
        for cp in part:
            cp.wait()


def per_device(cotangent, hot_ids, cold_owner, cold_slot, live_rows, hw, h1, h2, cw, c1, c2):
    vmem = pl.BlockSpec(memory_space=pltpu.VMEM)
    hbm = pl.BlockSpec(memory_space=pltpu.HBM)
    smem = pl.BlockSpec(memory_space=pltpu.SMEM)
    dma = pltpu.SemaphoreType.DMA
    bf16, f32, i32 = jnp.bfloat16, jnp.float32, jnp.int32
    state = (hw, h1, h2, cw, c1, c2)
    shapes = [jax.ShapeDtypeStruct(a.shape, a.dtype) for a in state]
    operands = (cotangent, hot_ids.T, cold_owner.T, cold_slot.T) + state
    staged = pl.pallas_call(
        comm_kernel,
        name="gradients",
        out_shape=[jax.ShapeDtypeStruct((NDP, 3, COLD_SHARE, HALF), bf16)] + shapes,
        in_specs=[hbm] * len(operands),
        out_specs=[vmem] * 7,
        scratch_shapes=[
            pltpu.VMEM((8, SAMP), i32),
            pltpu.VMEM((4, SAMP), i32),
            pltpu.VMEM((4, SAMP), i32),
            pltpu.VMEM((2, NDP, 8, SAMP), i32),
            pltpu.VMEM((2, NDP, SAMP, HALF), bf16),
            pltpu.VMEM((2, NY * NZ, SAMP), i32),
            pltpu.VMEM((2, CHUNKS, NY, PER * HOT_SHARE, SAMP), bf16),
            pltpu.VMEM((NY * NZ, SAMP), i32),
            pltpu.VMEM((2, CHUNKS, NY * BLOCK, NDP * SAMP), bf16),
            pltpu.VMEM((2, CHUNKS, NY * BLOCK, HALF), f32),
            pltpu.VMEM((2, CHUNKS, BLOCK, HALF), f32),
            pltpu.VMEM((2, CHUNKS, NY - 1, BLOCK, HALF), bf16),
            pltpu.VMEM((2, CHUNKS, NY - 1, BLOCK, HALF), bf16),
            pltpu.VMEM((len(KEPT), 3, COLD_SHARE, HALF), f32),
            pltpu.VMEM((NZ, 3, COLD_SHARE, HALF), bf16),
            pltpu.VMEM((NZ, 3, COLD_SHARE, HALF), bf16),
            pltpu.VMEM((len(FAR), 3, COLD_SHARE, HALF), bf16),
            pltpu.VMEM((NDP, 3, COLD_SHARE, HALF), bf16),
            dma((5,)),
            dma((6,)),
            dma((2, NDP)),
            dma((2, NDP)),
            dma((2, NX)),
            dma((2, NX)),
            dma((2, NDP)),
            dma((2, CHUNKS, NY - 1)),
            dma((2, CHUNKS, NY - 1)),
            dma((NZ,)),
            dma((NZ,)),
            dma((len(FAR),)),
            dma((NDP,)),
            dma((NDP,)),
            pltpu.SemaphoreType.REGULAR((2,)),
        ],
        compiler_params=pltpu.CompilerParams(collective_id=0, has_side_effects=True, vmem_limit_bytes=32 * 1024 * 1024),
    )(*(pltpu.with_memory_space_constraint(a, pltpu.HBM) for a in operands))
    return pl.pallas_call(
        adam_kernel,
        name="adam",
        out_shape=shapes,
        in_specs=[smem] + [vmem] * 7,
        out_specs=[hbm] * 6,
        scratch_shapes=[pltpu.VMEM(a.shape, a.dtype) for a in state] + [dma((3, 3))],
    )(live_rows, *(pltpu.with_memory_space_constraint(a, pltpu.VMEM) for a in staged))


def solution(mesh):
    rows = P(("dp", "table"), None)
    shard = P("table", None)
    return jax.shard_map(
        per_device, mesh=mesh, in_specs=(rows,) * 4 + (P("table"),) + (shard,) * 6, out_specs=(shard,) * 6,
        check_vma=False)
```

```python
import functools

import jax
import jax.numpy as jnp
from jax import lax
from jax.experimental import pallas as pl
from jax.experimental.pallas import tpu as pltpu
from jax.sharding import PartitionSpec as P

STEP = 3
BETA_ONE = 0.9
BETA_TWO = 0.999
ADAM_EPS = 1e-08
LEARN_RATE = 0.05
CLIP_NORM = 4.0

NX, NC, NY, NZ = 4, 2, 4, 16
SAMP = 256
FEAT = 256
HALF = FEAT // 2
HOT_LOCAL = 32
WINDOW = 256
TOUCHED = 128
NDP = NX * NC
HOT_SHARE = HOT_LOCAL // NDP
COLD_SHARE = TOUCHED // NDP
CHUNKS = 4
PER = NZ // CHUNKS
BLOCK = PER * (COLD_SHARE + HOT_SHARE)
Z_ORDER = [NZ // 2 + n // 2 if n % 2 == 0 else NZ // 2 - 1 - n // 2 for n in range(NZ)]
FOLD = 4
FAR = [r for r in Z_ORDER if FOLD < r < NZ - FOLD]
KEPT = [0, FOLD, NZ - FOLD]
LOGICAL = pl.DeviceIdType.MESH


def comm_kernel(
    cot_hbm, hot_hbm, owner_hbm, slot_hbm, s0, s1, s2, s3, s4, s5, out, o0, o1, o2, o3, o4, o5,
    hot_in, owner_in, slot_in, ids, cot, owner_rows, code_rows, slotfor, counts, part, psum_own, rsend, rrecv, zown,
    zsend, zrecv, zfar, fbuf,
    load_sem, state_sem, id_send, id_recv, cot_send, fwd_send, cot_recv, r_send, r_recv, z_send, z_recv, far_recv, f_send, f_recv,
    tokens,
):
    d = lax.axis_index("dp")
    t = lax.axis_index("table")
    x, c = d // NC, d % NC
    y, z = t // NZ, t % NZ

    def peer(axis, k, e=0):
        core = (1 - c) if e else c
        if axis == 0:
            return (lax.rem(x + k, NX) * NC + core, t)
        return (x * NC + core, lax.rem(y + k, NY) * NZ + z)

    def z_peer(r):
        return (d, y * NZ + lax.rem(z + r, NZ))

    partner = peer(0, 0, 1)
    offsets = [(k, e) for k in (2, 1, 3) for e in range(NC)]
    dp_peers = [partner] + [peer(0, k, e) for k, e in offsets]
    pending = []

    def send(src, dst, send_sem, recv_sem, device):
        cp = pltpu.make_async_remote_copy(
            src_ref=src, dst_ref=dst, send_sem=send_sem, recv_sem=recv_sem, device_id=device, device_id_type=LOGICAL)
        cp.start()
        pending.append(cp)

    def arrive(ref, recv_sem):
        pltpu.make_async_remote_copy(
            src_ref=ref, dst_ref=ref, send_sem=f_send.at[0], recv_sem=recv_sem, device_id=partner,
            device_id_type=LOGICAL).wait_recv()

    def signal(semaphore, device):
        pl.semaphore_signal(semaphore, inc=1, device_id=device, device_id_type=LOGICAL)

    loads = [
        pltpu.make_async_copy(hot_hbm, hot_in, load_sem.at[0]),
        pltpu.make_async_copy(owner_hbm, owner_in, load_sem.at[1]),
        pltpu.make_async_copy(slot_hbm, slot_in, load_sem.at[2]),
    ] + [
        pltpu.make_async_copy(cot_hbm.at[:, pl.ds(h * HALF, HALF)], cot.at[h, 0], load_sem.at[3 + h]) for h in range(2)
    ]
    for cp in loads:
        cp.start()
    barrier = pltpu.get_barrier_semaphore()
    near = [partner] + [peer(h, k) for h in range(2) for k in (2, 1, 3)] + [z_peer(r) for r in (1, 2, NZ - 2, NZ - 1)]
    for device in near:
        signal(barrier, device)
    states = [
        pltpu.make_async_copy(a, b, state_sem.at[i])
        for i, (a, b) in enumerate(zip((s0, s1, s2, s3, s4, s5), (o0, o1, o2, o3, o4, o5)))
    ]

    row = lax.broadcasted_iota(jnp.int32, (NY * NZ, SAMP), 0)
    order = (row // (NY * PER)) * PER + row % PER
    zrel = jnp.where(order % 2 == 0, NZ // 2 + order // 2, NZ // 2 - 1 - order // 2)
    yrel = (row // PER) % NY
    owner_rows[0] = ((y + yrel) % NY) * NZ + (z + zrel) % NZ
    owner_rows[1] = y * NZ + (z + zrel) % NZ
    i = lax.broadcasted_iota(jnp.int32, (PER * HOT_SHARE, SAMP), 0)
    for q in range(CHUNKS):
        n = q * PER + i // HOT_SHARE
        rel = jnp.where(n % 2 == 0, NZ // 2 + n // 2, NZ // 2 - 1 - n // 2)
        zz = (z + rel) % NZ
        for r in range(NY):
            first = (((y + r) % NY) * NZ + zz) * HOT_SHARE + i % HOT_SHARE
            second = (zz * NX + (x + r) % NX) * HOT_SHARE + i % HOT_SHARE
            code_rows[0, q, r] = first.astype(jnp.float32).astype(jnp.bfloat16)
            code_rows[1, q, r] = second.astype(jnp.float32).astype(jnp.bfloat16)
    lanes = lax.broadcasted_iota(jnp.int32, (COLD_SHARE, SAMP), 0)

    def build(h, source, g):
        block = ids[source, g]
        lo = block & 65535
        hi = block // 65536
        value = jnp.full((NY * NZ, SAMP), -1, jnp.int32)
        owners = owner_rows[h]
        for v in (lo[4:5], lo[5:6], hi[4:5], hi[5:6]):
            value = jnp.where(v // TOUCHED == owners, v % TOUCHED, value)
        slotfor[...] = value
        hot_ids = []
        for words in (lo, hi):
            shard = words[0:4] // HOT_LOCAL
            share = (words[0:4] % HOT_LOCAL) // HOT_SHARE
            inner = words[0:4] % HOT_SHARE
            if h == 0:
                code = jnp.where(share == d, shard * HOT_SHARE + inner, -1)
            else:
                code = ((shard % NZ) * NX + share // NC) * HOT_SHARE + inner
                code = jnp.where((shard // NZ == y) & (share % NC == c), code, -1)
            for j in range(4):
                wide = jnp.broadcast_to(code[j:j + 1], (PER * HOT_SHARE, SAMP))
                hot_ids.append(wide.astype(jnp.float32).astype(jnp.bfloat16))
        columns = pl.ds(pl.multiple_of(g * SAMP, SAMP), SAMP)
        for q in range(CHUNKS):
            for r in range(NY):
                share = d if h == 0 else lax.rem(x + r, NX) * NC + c
                slots = lanes + share * COLD_SHARE
                for k in range(PER):
                    ell = (q * NY + r) * PER + k
                    match = slotfor[ell:ell + 1, :] == slots
                    counts[h, q, pl.ds(r * BLOCK + k * COLD_SHARE, COLD_SHARE), columns] = jnp.where(match, 1.0, 0.0).astype(jnp.bfloat16)
                codes = code_rows[h, q, r]
                total = jnp.zeros((PER * HOT_SHARE, SAMP), jnp.bfloat16)
                for v in hot_ids:
                    total = total + jnp.where(v == codes, jnp.bfloat16(1), jnp.bfloat16(0))
                counts[h, q, pl.ds(r * BLOCK + PER * COLD_SHARE, PER * HOT_SHARE), columns] = total

    for cp in loads[:3]:
        cp.wait()
    hot = hot_in[...]
    cold = owner_in[...] * TOUCHED + slot_in[...]
    ids[0, 0, 0:4, :] = hot[0:4] + hot[4:8] * 65536
    ids[0, 0, 4:6, :] = cold[0:2] + cold[2:4] * 65536
    ids[0, 0, 6:8, :] = jnp.zeros((2, SAMP), jnp.int32)
    for cp in loads[3:]:
        cp.wait()
    for h in range(2):
        build(h, 0, 0)

    pl.semaphore_wait(barrier, len(near))

    send(ids.at[0, 0], ids.at[0, NX], id_send.at[0, NX], id_recv.at[0, NX], partner)
    for k in (2, 1, 3):
        for h in range(2):
            send(ids.at[0, 0], ids.at[h, NX - k], id_send.at[h, NX - k], id_recv.at[h, NX - k], peer(h, k))

    def forward(h, k):
        send(cot.at[h, k], cot.at[h, NX + k], fwd_send.at[h, k], cot_recv.at[h, NX + k], partner)

    for k in (2, 1, 3):
        for h in range(2):
            send(cot.at[h, 0], cot.at[h, NX - k], cot_send.at[h, k], cot_recv.at[h, NX - k], peer(h, k))
    for h in range(2):
        forward(h, 0)
    for r, i in ((2, 1), (NZ - 2, 0)):
        signal(tokens.at[i], z_peer(r))

    arrive(ids.at[0, NX], id_recv.at[0, NX])
    for h in range(2):
        build(h, 0, NX)
    for k in (1, 3, 2):
        for h in range(2):
            arrive(ids.at[h, k], id_recv.at[h, k])
            send(ids.at[h, k], ids.at[h, NX + k], id_send.at[h, NX + k], id_recv.at[h, NX + k], partner)

    for h in range(2):
        def build_mine(k, carry):
            build(h, h, k)
            return carry

        lax.fori_loop(1, NX, build_mine, 0)
    for h in range(2):
        def build_other(k, carry):
            arrive(ids.at[h, NX + k], id_recv.at[h, NX + k])
            build(h, h, NX + k)
            return carry

        lax.fori_loop(1, NX, build_other, 0)

    for k in (2, 1, 3):
        for h in range(2):
            arrive(cot.at[h, k], cot_recv.at[h, k])
            forward(h, k)
    for cp in states:
        cp.start()

    def product(h, q, first):
        left = counts[h, q, :, first * SAMP:(first + NX) * SAMP]
        right = cot[h, first:first + NX].reshape(NX * SAMP, HALF)
        return jnp.dot(left, right, preferred_element_type=jnp.float32)

    ahead = 2
    for q in range(ahead):
        for h in range(2):
            part[h, q] = product(h, q, 0)
    for k in (0, 2, 1, 3):
        for h in range(2):
            arrive(cot.at[h, NX + k], cot_recv.at[h, NX + k])
    for q in range(CHUNKS):
        for h in range(2):
            done = (part[h, q] if q < ahead else product(h, q, 0)) + product(h, q, NX)
            psum_own[h, q] = done[0:BLOCK]
            for r in (2, 1, 3):
                rsend[h, q, r - 1] = done[r * BLOCK:(r + 1) * BLOCK].astype(jnp.bfloat16)
                there = NY - 1 - r
                send(rsend.at[h, q, r - 1], rrecv.at[h, q, there], r_send.at[h, q, r - 1], r_recv.at[h, q, there], peer(1 - h, r))

    pl.semaphore_wait(tokens.at[0], 1)
    pl.semaphore_wait(tokens.at[1], 1)
    for q in range(CHUNKS):
        totals = []
        for h in range(2):
            total = psum_own[h, q]
            for r in (0, 2, 1):
                arrive(rrecv.at[h, q, r], r_recv.at[h, q, r])
                total = total + rrecv[h, q, r].astype(jnp.float32)
            totals.append(total)
        for k in range(PER):
            n = q * PER + k
            rel = Z_ORDER[n]
            cold_rows = slice(k * COLD_SHARE, (k + 1) * COLD_SHARE)
            base = PER * COLD_SHARE + k * HOT_SHARE
            hot_parts = [total[base:base + HOT_SHARE] for total in totals]
            packed = [total[cold_rows] for total in totals] + [
                jnp.concatenate(hot_parts + [jnp.zeros((8, HALF), jnp.float32)], axis=0)]
            if rel in KEPT:
                for i in range(3):
                    zown[KEPT.index(rel), i] = packed[i]
                continue
            for i in range(3):
                zsend[n, i] = packed[i].astype(jnp.bfloat16)
            if rel in FAR:
                send(zsend.at[n], zfar.at[FAR.index(rel)], z_send.at[n], far_recv.at[FAR.index(rel)],
                     z_peer(rel - FOLD if rel <= NZ // 2 else rel + FOLD))
            else:
                there = Z_ORDER.index(NZ - rel)
                send(zsend.at[n], zrecv.at[there], z_send.at[n], z_recv.at[there], z_peer(rel))

    for rel in (FOLD, NZ - FOLD):
        total = [zown[KEPT.index(rel), i] for i in range(3)]
        for far in FAR:
            if (far <= NZ // 2) == (rel == FOLD):
                arrive(zfar.at[FAR.index(far)], far_recv.at[FAR.index(far)])
                total = [total[i] + zfar[FAR.index(far), i].astype(jnp.float32) for i in range(3)]
        n, there = Z_ORDER.index(rel), Z_ORDER.index(NZ - rel)
        for i in range(3):
            zsend[n, i] = total[i].astype(jnp.bfloat16)
        send(zsend.at[n], zrecv.at[there], z_send.at[n], z_recv.at[there], z_peer(rel))
    while pending:
        pending.pop(0).wait_send()

    total = [zown[0, i] for i in range(3)]
    for rel in (1, NZ - 1, 2, NZ - 2, 3, NZ - 3, FOLD, NZ - FOLD):
        n = Z_ORDER.index(rel)
        arrive(zrecv.at[n], z_recv.at[n])
        total = [total[i] + zrecv[n, i].astype(jnp.float32) for i in range(3)]
    for i in range(3):
        fbuf[d, i] = total[i].astype(jnp.bfloat16)
    for i, device in enumerate(dp_peers):
        send(fbuf.at[d], fbuf.at[d], f_send.at[i], f_recv.at[d], device)
    for cp in states:
        cp.wait()
    for device in dp_peers:
        arrive(fbuf.at[device[0]], f_recv.at[device[0]])
    out[...] = fbuf[...]
    for cp in pending:
        cp.wait_send()


def adam(weight, one, two, gradient):
    row_norm = jnp.sqrt(jnp.sum(gradient * gradient, axis=1, keepdims=True))
    clipped = gradient * (CLIP_NORM / jnp.maximum(row_norm, CLIP_NORM))
    first = BETA_ONE * one + (1.0 - BETA_ONE) * clipped
    second = BETA_TWO * two + (1.0 - BETA_TWO) * clipped * clipped
    correct_one = 1.0 - BETA_ONE**STEP
    correct_two = 1.0 - BETA_TWO**STEP
    stepped = weight - LEARN_RATE * (first / correct_one) / (jnp.sqrt(second / correct_two) + ADAM_EPS)
    return stepped, first, second


def adam_kernel(live, grads, *refs):
    held, news, made, store_sem = refs[0:6], refs[6:12], refs[12:18], refs[18]
    whole = slice(None)
    parts = [(3, slice(TOUCHED, WINDOW)), (0, whole), (3, slice(0, TOUCHED))]
    stores = [
        [pltpu.make_async_copy(made[a + i].at[rows], news[a + i].at[rows], store_sem.at[p, i]) for i in range(3)]
        for p, (a, rows) in enumerate(parts)
    ]
    count = live[0]

    def cold(rows, start, gradient):
        old = [held[3 + i][rows, :] for i in range(3)]
        new = adam(*old, gradient)
        active = lax.broadcasted_iota(jnp.int32, gradient.shape, 0) + start < count
        for i in range(3):
            made[3 + i][rows, :] = jnp.where(active, new[i], old[i])

    for start in range(TOUCHED, WINDOW, 32):
        cold(slice(start, start + 32), start, jnp.zeros((32, FEAT), jnp.float32))
    for cp in stores[0]:
        cp.start()

    tiles = [grads[d, 2].astype(jnp.float32) for d in range(NDP)]
    left = jnp.concatenate([tile[0:HOT_SHARE] for tile in tiles], axis=0)
    right = jnp.concatenate([tile[HOT_SHARE:2 * HOT_SHARE] for tile in tiles], axis=0)
    new = adam(held[0][...], held[1][...], held[2][...], jnp.concatenate([left, right], axis=1))
    for i in range(3):
        made[i][...] = new[i]
    for cp in stores[1]:
        cp.start()

    for d in range(NDP):
        gradient = jnp.concatenate([grads[d, 0], grads[d, 1]], axis=1).astype(jnp.float32)
        cold(slice(d * COLD_SHARE, (d + 1) * COLD_SHARE), d * COLD_SHARE, gradient)
    for cp in stores[2]:
        cp.start()
    for part in stores:
        for cp in part:
            cp.wait()


def per_device(cotangent, hot_ids, cold_owner, cold_slot, live_rows, hw, h1, h2, cw, c1, c2):
    vmem = pl.BlockSpec(memory_space=pltpu.VMEM)
    hbm = pl.BlockSpec(memory_space=pltpu.HBM)
    smem = pl.BlockSpec(memory_space=pltpu.SMEM)
    dma = pltpu.SemaphoreType.DMA
    bf16, f32, i32 = jnp.bfloat16, jnp.float32, jnp.int32
    state = (hw, h1, h2, cw, c1, c2)
    shapes = [jax.ShapeDtypeStruct(a.shape, a.dtype) for a in state]
    operands = (cotangent, hot_ids.T, cold_owner.T, cold_slot.T) + state
    staged = pl.pallas_call(
        comm_kernel,
        name="gradients",
        out_shape=[jax.ShapeDtypeStruct((NDP, 3, COLD_SHARE, HALF), bf16)] + shapes,
        in_specs=[hbm] * len(operands),
        out_specs=[vmem] * 7,
        scratch_shapes=[
            pltpu.VMEM((8, SAMP), i32),
            pltpu.VMEM((4, SAMP), i32),
            pltpu.VMEM((4, SAMP), i32),
            pltpu.VMEM((2, NDP, 8, SAMP), i32),
            pltpu.VMEM((2, NDP, SAMP, HALF), bf16),
            pltpu.VMEM((2, NY * NZ, SAMP), i32),
            pltpu.VMEM((2, CHUNKS, NY, PER * HOT_SHARE, SAMP), bf16),
            pltpu.VMEM((NY * NZ, SAMP), i32),
            pltpu.VMEM((2, CHUNKS, NY * BLOCK, NDP * SAMP), bf16),
            pltpu.VMEM((2, CHUNKS, NY * BLOCK, HALF), f32),
            pltpu.VMEM((2, CHUNKS, BLOCK, HALF), f32),
            pltpu.VMEM((2, CHUNKS, NY - 1, BLOCK, HALF), bf16),
            pltpu.VMEM((2, CHUNKS, NY - 1, BLOCK, HALF), bf16),
            pltpu.VMEM((len(KEPT), 3, COLD_SHARE, HALF), f32),
            pltpu.VMEM((NZ, 3, COLD_SHARE, HALF), bf16),
            pltpu.VMEM((NZ, 3, COLD_SHARE, HALF), bf16),
            pltpu.VMEM((len(FAR), 3, COLD_SHARE, HALF), bf16),
            pltpu.VMEM((NDP, 3, COLD_SHARE, HALF), bf16),
            dma((5,)),
            dma((6,)),
            dma((2, NDP)),
            dma((2, NDP)),
            dma((2, NX)),
            dma((2, NX)),
            dma((2, NDP)),
            dma((2, CHUNKS, NY - 1)),
            dma((2, CHUNKS, NY - 1)),
            dma((NZ,)),
            dma((NZ,)),
            dma((len(FAR),)),
            dma((NDP,)),
            dma((NDP,)),
            pltpu.SemaphoreType.REGULAR((2,)),
        ],
        compiler_params=pltpu.CompilerParams(collective_id=0, has_side_effects=True, vmem_limit_bytes=32 * 1024 * 1024),
    )(*(pltpu.with_memory_space_constraint(a, pltpu.HBM) for a in operands))
    return pl.pallas_call(
        adam_kernel,
        name="adam",
        out_shape=shapes,
        in_specs=[smem] + [vmem] * 7,
        out_specs=[hbm] * 6,
        scratch_shapes=[pltpu.VMEM(a.shape, a.dtype) for a in state] + [dma((3, 3))],
    )(live_rows, *(pltpu.with_memory_space_constraint(a, pltpu.VMEM) for a in staged))


def solution(mesh):
    rows = P(("dp", "table"), None)
    shard = P("table", None)
    return jax.shard_map(
        per_device, mesh=mesh, in_specs=(rows,) * 4 + (P("table"),) + (shard,) * 6, out_specs=(shard,) * 6,
        check_vma=False)
```

```python
import functools

import jax
import jax.numpy as jnp
from jax import lax
from jax.experimental import pallas as pl
from jax.experimental.pallas import tpu as pltpu
from jax.sharding import PartitionSpec as P

STEP = 3
BETA_ONE = 0.9
BETA_TWO = 0.999
ADAM_EPS = 1e-08
LEARN_RATE = 0.05
CLIP_NORM = 4.0

NX, NC, NY, NZ = 4, 2, 4, 16
SAMP = 256
FEAT = 256
HALF = FEAT // 2
HOT_LOCAL = 32
WINDOW = 256
TOUCHED = 128
NDP = NX * NC
HOT_SHARE = HOT_LOCAL // NDP
COLD_SHARE = TOUCHED // NDP
CHUNKS = 4
PER = NZ // CHUNKS
BLOCK = PER * (COLD_SHARE + HOT_SHARE)
Z_ORDER = [NZ // 2 + n // 2 if n % 2 == 0 else NZ // 2 - 1 - n // 2 for n in range(NZ)]
FOLD = 4
FAR = [r for r in Z_ORDER if FOLD < r < NZ - FOLD]
KEPT = [0, FOLD, NZ - FOLD]
LOGICAL = pl.DeviceIdType.MESH


def comm_kernel(
    cot_hbm, hot_hbm, owner_hbm, slot_hbm, s0, s1, s2, s3, s4, s5, out, o0, o1, o2, o3, o4, o5,
    hot_in, owner_in, slot_in, ids, cot, owner_rows, code_rows, slotfor, counts, part, psum_own, rsend, rrecv, zown,
    zsend, zrecv, zfar, fbuf,
    load_sem, state_sem, id_send, id_recv, cot_send, fwd_send, cot_recv, r_send, r_recv, z_send, z_recv, far_recv, f_send, f_recv,
    tokens,
):
    d = lax.axis_index("dp")
    t = lax.axis_index("table")
    x, c = d // NC, d % NC
    y, z = t // NZ, t % NZ

    def peer(axis, k, e=0):
        core = (1 - c) if e else c
        if axis == 0:
            return (lax.rem(x + k, NX) * NC + core, t)
        return (x * NC + core, lax.rem(y + k, NY) * NZ + z)

    def z_peer(r):
        return (d, y * NZ + lax.rem(z + r, NZ))

    partner = peer(0, 0, 1)
    offsets = [(k, e) for k in (2, 1, 3) for e in range(NC)]
    dp_peers = [partner] + [peer(0, k, e) for k, e in offsets]
    pending = []

    def send(src, dst, send_sem, recv_sem, device):
        cp = pltpu.make_async_remote_copy(
            src_ref=src, dst_ref=dst, send_sem=send_sem, recv_sem=recv_sem, device_id=device, device_id_type=LOGICAL)
        cp.start()
        pending.append(cp)

    def arrive(ref, recv_sem):
        pltpu.make_async_remote_copy(
            src_ref=ref, dst_ref=ref, send_sem=f_send.at[0], recv_sem=recv_sem, device_id=partner,
            device_id_type=LOGICAL).wait_recv()

    def signal(semaphore, device):
        pl.semaphore_signal(semaphore, inc=1, device_id=device, device_id_type=LOGICAL)

    loads = [
        pltpu.make_async_copy(hot_hbm, hot_in, load_sem.at[0]),
        pltpu.make_async_copy(owner_hbm, owner_in, load_sem.at[1]),
        pltpu.make_async_copy(slot_hbm, slot_in, load_sem.at[2]),
    ] + [
        pltpu.make_async_copy(cot_hbm.at[:, pl.ds(h * HALF, HALF)], cot.at[h, 0], load_sem.at[3 + h]) for h in range(2)
    ]
    for cp in loads:
        cp.start()
    barrier = pltpu.get_barrier_semaphore()
    near = [partner] + [peer(h, k) for h in range(2) for k in (2, 1, 3)] + [z_peer(r) for r in (1, 2, NZ - 2, NZ - 1)]
    for device in near:
        signal(barrier, device)
    states = [
        pltpu.make_async_copy(a, b, state_sem.at[i])
        for i, (a, b) in enumerate(zip((s0, s1, s2, s3, s4, s5), (o0, o1, o2, o3, o4, o5)))
    ]

    row = lax.broadcasted_iota(jnp.int32, (NY * NZ, SAMP), 0)
    order = (row // (NY * PER)) * PER + row % PER
    zrel = jnp.where(order % 2 == 0, NZ // 2 + order // 2, NZ // 2 - 1 - order // 2)
    yrel = (row // PER) % NY
    owner_rows[0] = ((y + yrel) % NY) * NZ + (z + zrel) % NZ
    owner_rows[1] = y * NZ + (z + zrel) % NZ
    i = lax.broadcasted_iota(jnp.int32, (PER * HOT_SHARE, SAMP), 0)
    for q in range(CHUNKS):
        n = q * PER + i // HOT_SHARE
        rel = jnp.where(n % 2 == 0, NZ // 2 + n // 2, NZ // 2 - 1 - n // 2)
        zz = (z + rel) % NZ
        for r in range(NY):
            first = (((y + r) % NY) * NZ + zz) * HOT_SHARE + i % HOT_SHARE
            second = (zz * NX + (x + r) % NX) * HOT_SHARE + i % HOT_SHARE
            code_rows[0, q, r] = first.astype(jnp.float32).astype(jnp.bfloat16)
            code_rows[1, q, r] = second.astype(jnp.float32).astype(jnp.bfloat16)
    lanes = lax.broadcasted_iota(jnp.int32, (COLD_SHARE, SAMP), 0)

    def build(h, source, g):
        block = ids[source, g]
        lo = block & 65535
        hi = block // 65536
        value = jnp.full((NY * NZ, SAMP), -1, jnp.int32)
        owners = owner_rows[h]
        for v in (lo[4:5], lo[5:6], hi[4:5], hi[5:6]):
            value = jnp.where(v // TOUCHED == owners, v % TOUCHED, value)
        slotfor[...] = value
        hot_ids = []
        for words in (lo, hi):
            shard = words[0:4] // HOT_LOCAL
            share = (words[0:4] % HOT_LOCAL) // HOT_SHARE
            inner = words[0:4] % HOT_SHARE
            if h == 0:
                code = jnp.where(share == d, shard * HOT_SHARE + inner, -1)
            else:
                code = ((shard % NZ) * NX + share // NC) * HOT_SHARE + inner
                code = jnp.where((shard // NZ == y) & (share % NC == c), code, -1)
            for j in range(4):
                wide = jnp.broadcast_to(code[j:j + 1], (PER * HOT_SHARE, SAMP))
                hot_ids.append(wide.astype(jnp.float32).astype(jnp.bfloat16))
        columns = pl.ds(pl.multiple_of(g * SAMP, SAMP), SAMP)
        for q in range(CHUNKS):
            for r in range(NY):
                share = d if h == 0 else lax.rem(x + r, NX) * NC + c
                slots = lanes + share * COLD_SHARE
                for k in range(PER):
                    ell = (q * NY + r) * PER + k
                    match = slotfor[ell:ell + 1, :] == slots
                    counts[h, q, pl.ds(r * BLOCK + k * COLD_SHARE, COLD_SHARE), columns] = jnp.where(match, 1.0, 0.0).astype(jnp.bfloat16)
                codes = code_rows[h, q, r]
                total = jnp.zeros((PER * HOT_SHARE, SAMP), jnp.bfloat16)
                for v in hot_ids:
                    total = total + jnp.where(v == codes, jnp.bfloat16(1), jnp.bfloat16(0))
                counts[h, q, pl.ds(r * BLOCK + PER * COLD_SHARE, PER * HOT_SHARE), columns] = total

    for cp in loads[:3]:
        cp.wait()
    hot = hot_in[...]
    cold = owner_in[...] * TOUCHED + slot_in[...]
    ids[0, 0, 0:4, :] = hot[0:4] + hot[4:8] * 65536
    ids[0, 0, 4:6, :] = cold[0:2] + cold[2:4] * 65536
    ids[0, 0, 6:8, :] = jnp.zeros((2, SAMP), jnp.int32)
    for cp in loads[3:]:
        cp.wait()
    for h in range(2):
        build(h, 0, 0)

    pl.semaphore_wait(barrier, len(near))

    send(ids.at[0, 0], ids.at[0, NX], id_send.at[0, NX], id_recv.at[0, NX], partner)
    for k in (2, 1, 3):
        for h in range(2):
            send(ids.at[0, 0], ids.at[h, NX - k], id_send.at[h, NX - k], id_recv.at[h, NX - k], peer(h, k))

    def forward(h, k):
        send(cot.at[h, k], cot.at[h, NX + k], fwd_send.at[h, k], cot_recv.at[h, NX + k], partner)

    for k in (2, 1, 3):
        for h in range(2):
            send(cot.at[h, 0], cot.at[h, NX - k], cot_send.at[h, k], cot_recv.at[h, NX - k], peer(h, k))
    for h in range(2):
        forward(h, 0)
    for r, i in ((2, 1), (NZ - 2, 0)):
        signal(tokens.at[i], z_peer(r))

    arrive(ids.at[0, NX], id_recv.at[0, NX])
    for h in range(2):
        build(h, 0, NX)
    for k in (1, 3, 2):
        for h in range(2):
            arrive(ids.at[h, k], id_recv.at[h, k])
            send(ids.at[h, k], ids.at[h, NX + k], id_send.at[h, NX + k], id_recv.at[h, NX + k], partner)

    for h in range(2):
        def build_mine(k, carry):
            build(h, h, k)
            return carry

        lax.fori_loop(1, NX, build_mine, 0)
    for h in range(2):
        def build_other(k, carry):
            arrive(ids.at[h, NX + k], id_recv.at[h, NX + k])
            build(h, h, NX + k)
            return carry

        lax.fori_loop(1, NX, build_other, 0)

    for k in (1, 3, 2):
        for h in range(2):
            arrive(cot.at[h, k], cot_recv.at[h, k])
            forward(h, k)
    for cp in states:
        cp.start()

    middle = NX * SAMP
    for h in range(2):
        mine = cot[h, 0:NX].reshape(middle, HALF)
        for q in range(CHUNKS):
            part[h, q] = jnp.dot(counts[h, q, :, 0:middle], mine, preferred_element_type=jnp.float32)
    for h in range(2):
        for k in (0, 1, 3, 2):
            arrive(cot.at[h, NX + k], cot_recv.at[h, NX + k])
    for q in range(CHUNKS):
        for h in range(2):
            others = cot[h, NX:NDP].reshape(middle, HALF)
            done = part[h, q] + jnp.dot(counts[h, q, :, middle:2 * middle], others, preferred_element_type=jnp.float32)
            psum_own[h, q] = done[0:BLOCK]
            for r in (2, 1, 3):
                rsend[h, q, r - 1] = done[r * BLOCK:(r + 1) * BLOCK].astype(jnp.bfloat16)
                there = NY - 1 - r
                send(rsend.at[h, q, r - 1], rrecv.at[h, q, there], r_send.at[h, q, r - 1], r_recv.at[h, q, there], peer(1 - h, r))

    pl.semaphore_wait(tokens.at[0], 1)
    pl.semaphore_wait(tokens.at[1], 1)
    for q in range(CHUNKS):
        totals = []
        for h in range(2):
            total = psum_own[h, q]
            for r in (0, 2, 1):
                arrive(rrecv.at[h, q, r], r_recv.at[h, q, r])
                total = total + rrecv[h, q, r].astype(jnp.float32)
            totals.append(total)
        for k in range(PER):
            n = q * PER + k
            rel = Z_ORDER[n]
            cold_rows = slice(k * COLD_SHARE, (k + 1) * COLD_SHARE)
            base = PER * COLD_SHARE + k * HOT_SHARE
            hot_parts = [total[base:base + HOT_SHARE] for total in totals]
            packed = [total[cold_rows] for total in totals] + [
                jnp.concatenate(hot_parts + [jnp.zeros((8, HALF), jnp.float32)], axis=0)]
            if rel in KEPT:
                for i in range(3):
                    zown[KEPT.index(rel), i] = packed[i]
                continue
            for i in range(3):
                zsend[n, i] = packed[i].astype(jnp.bfloat16)
            if rel in FAR:
                send(zsend.at[n], zfar.at[FAR.index(rel)], z_send.at[n], far_recv.at[FAR.index(rel)],
                     z_peer(rel - FOLD if rel <= NZ // 2 else rel + FOLD))
            else:
                there = Z_ORDER.index(NZ - rel)
                send(zsend.at[n], zrecv.at[there], z_send.at[n], z_recv.at[there], z_peer(rel))

    for rel in (FOLD, NZ - FOLD):
        total = [zown[KEPT.index(rel), i] for i in range(3)]
        for far in FAR:
            if (far <= NZ // 2) == (rel == FOLD):
                arrive(zfar.at[FAR.index(far)], far_recv.at[FAR.index(far)])
                total = [total[i] + zfar[FAR.index(far), i].astype(jnp.float32) for i in range(3)]
        n, there = Z_ORDER.index(rel), Z_ORDER.index(NZ - rel)
        for i in range(3):
            zsend[n, i] = total[i].astype(jnp.bfloat16)
        send(zsend.at[n], zrecv.at[there], z_send.at[n], z_recv.at[there], z_peer(rel))
    while pending:
        pending.pop(0).wait_send()

    total = [zown[0, i] for i in range(3)]
    for rel in (1, NZ - 1, 2, NZ - 2, 3, NZ - 3, FOLD, NZ - FOLD):
        n = Z_ORDER.index(rel)
        arrive(zrecv.at[n], z_recv.at[n])
        total = [total[i] + zrecv[n, i].astype(jnp.float32) for i in range(3)]
    for i in range(3):
        fbuf[d, i] = total[i].astype(jnp.bfloat16)
    for i, device in enumerate(dp_peers):
        send(fbuf.at[d], fbuf.at[d], f_send.at[i], f_recv.at[d], device)
    for cp in states:
        cp.wait()
    for device in dp_peers:
        arrive(fbuf.at[device[0]], f_recv.at[device[0]])
    out[...] = fbuf[...]
    for cp in pending:
        cp.wait_send()


def adam(weight, one, two, gradient):
    row_norm = jnp.sqrt(jnp.sum(gradient * gradient, axis=1, keepdims=True))
    clipped = gradient * (CLIP_NORM / jnp.maximum(row_norm, CLIP_NORM))
    first = BETA_ONE * one + (1.0 - BETA_ONE) * clipped
    second = BETA_TWO * two + (1.0 - BETA_TWO) * clipped * clipped
    correct_one = 1.0 - BETA_ONE**STEP
    correct_two = 1.0 - BETA_TWO**STEP
    stepped = weight - LEARN_RATE * (first / correct_one) / (jnp.sqrt(second / correct_two) + ADAM_EPS)
    return stepped, first, second


def adam_kernel(live, grads, *refs):
    held, news, made, store_sem = refs[0:6], refs[6:12], refs[12:18], refs[18]
    whole = slice(None)
    parts = [(3, slice(TOUCHED, WINDOW)), (0, whole), (3, slice(0, TOUCHED))]
    stores = [
        [pltpu.make_async_copy(made[a + i].at[rows], news[a + i].at[rows], store_sem.at[p, i]) for i in range(3)]
        for p, (a, rows) in enumerate(parts)
    ]
    count = live[0]

    def cold(rows, start, gradient):
        old = [held[3 + i][rows, :] for i in range(3)]
        new = adam(*old, gradient)
        active = lax.broadcasted_iota(jnp.int32, gradient.shape, 0) + start < count
        for i in range(3):
            made[3 + i][rows, :] = jnp.where(active, new[i], old[i])

    for start in range(TOUCHED, WINDOW, 32):
        cold(slice(start, start + 32), start, jnp.zeros((32, FEAT), jnp.float32))
    for cp in stores[0]:
        cp.start()

    tiles = [grads[d, 2].astype(jnp.float32) for d in range(NDP)]
    left = jnp.concatenate([tile[0:HOT_SHARE] for tile in tiles], axis=0)
    right = jnp.concatenate([tile[HOT_SHARE:2 * HOT_SHARE] for tile in tiles], axis=0)
    new = adam(held[0][...], held[1][...], held[2][...], jnp.concatenate([left, right], axis=1))
    for i in range(3):
        made[i][...] = new[i]
    for cp in stores[1]:
        cp.start()

    for d in range(NDP):
        gradient = jnp.concatenate([grads[d, 0], grads[d, 1]], axis=1).astype(jnp.float32)
        cold(slice(d * COLD_SHARE, (d + 1) * COLD_SHARE), d * COLD_SHARE, gradient)
    for cp in stores[2]:
        cp.start()
    for part in stores:
        for cp in part:
            cp.wait()


def per_device(cotangent, hot_ids, cold_owner, cold_slot, live_rows, hw, h1, h2, cw, c1, c2):
    vmem = pl.BlockSpec(memory_space=pltpu.VMEM)
    hbm = pl.BlockSpec(memory_space=pltpu.HBM)
    smem = pl.BlockSpec(memory_space=pltpu.SMEM)
    dma = pltpu.SemaphoreType.DMA
    bf16, f32, i32 = jnp.bfloat16, jnp.float32, jnp.int32
    state = (hw, h1, h2, cw, c1, c2)
    shapes = [jax.ShapeDtypeStruct(a.shape, a.dtype) for a in state]
    operands = (cotangent, hot_ids.T, cold_owner.T, cold_slot.T) + state
    staged = pl.pallas_call(
        comm_kernel,
        name="gradients",
        out_shape=[jax.ShapeDtypeStruct((NDP, 3, COLD_SHARE, HALF), bf16)] + shapes,
        in_specs=[hbm] * len(operands),
        out_specs=[vmem] * 7,
        scratch_shapes=[
            pltpu.VMEM((8, SAMP), i32),
            pltpu.VMEM((4, SAMP), i32),
            pltpu.VMEM((4, SAMP), i32),
            pltpu.VMEM((2, NDP, 8, SAMP), i32),
            pltpu.VMEM((2, NDP, SAMP, HALF), bf16),
            pltpu.VMEM((2, NY * NZ, SAMP), i32),
            pltpu.VMEM((2, CHUNKS, NY, PER * HOT_SHARE, SAMP), bf16),
            pltpu.VMEM((NY * NZ, SAMP), i32),
            pltpu.VMEM((2, CHUNKS, NY * BLOCK, NDP * SAMP), bf16),
            pltpu.VMEM((2, CHUNKS, NY * BLOCK, HALF), f32),
            pltpu.VMEM((2, CHUNKS, BLOCK, HALF), f32),
            pltpu.VMEM((2, CHUNKS, NY - 1, BLOCK, HALF), bf16),
            pltpu.VMEM((2, CHUNKS, NY - 1, BLOCK, HALF), bf16),
            pltpu.VMEM((len(KEPT), 3, COLD_SHARE, HALF), f32),
            pltpu.VMEM((NZ, 3, COLD_SHARE, HALF), bf16),
            pltpu.VMEM((NZ, 3, COLD_SHARE, HALF), bf16),
            pltpu.VMEM((len(FAR), 3, COLD_SHARE, HALF), bf16),
            pltpu.VMEM((NDP, 3, COLD_SHARE, HALF), bf16),
            dma((5,)),
            dma((6,)),
            dma((2, NDP)),
            dma((2, NDP)),
            dma((2, NX)),
            dma((2, NX)),
            dma((2, NDP)),
            dma((2, CHUNKS, NY - 1)),
            dma((2, CHUNKS, NY - 1)),
            dma((NZ,)),
            dma((NZ,)),
            dma((len(FAR),)),
            dma((NDP,)),
            dma((NDP,)),
            pltpu.SemaphoreType.REGULAR((2,)),
        ],
        compiler_params=pltpu.CompilerParams(collective_id=0, has_side_effects=True, vmem_limit_bytes=32 * 1024 * 1024),
    )(*(pltpu.with_memory_space_constraint(a, pltpu.HBM) for a in operands))
    return pl.pallas_call(
        adam_kernel,
        name="adam",
        out_shape=shapes,
        in_specs=[smem] + [vmem] * 7,
        out_specs=[hbm] * 6,
        scratch_shapes=[pltpu.VMEM(a.shape, a.dtype) for a in state] + [dma((3, 3))],
    )(live_rows, *(pltpu.with_memory_space_constraint(a, pltpu.VMEM) for a in staged))


def solution(mesh):
    rows = P(("dp", "table"), None)
    shard = P("table", None)
    return jax.shard_map(
        per_device, mesh=mesh, in_specs=(rows,) * 4 + (P("table"),) + (shard,) * 6, out_specs=(shard,) * 6,
        check_vma=False)
```
